256 devices in a mesh: chan: 64 (over z_lo, x, y, core), space: 4 (over z_hi).
Axes of the slice: x: 4, y: 4, z: 8 (z_hi: 4, z_lo: 2; z = z_hi * 2 + z_lo), core: 2. Of those that a mesh axis runs over, the one named last changes fastest.
Arguments:
- volume: float32 [96, 128, 64, 128], P(None, 'chan', 'space'), may hold values from -6 to 6
- filters: float32 [27, 9216], replicated, may hold values from -0.125 to 0.125
- offsets: float32 [96], replicated, may hold values from -3 to 3
- upstream: float32 [96, 128, 64, 128], P(None, 'chan', 'space'), may hold values from -6 to 6
Outputs:
- response: float32 [96, 128, 64, 128], P(None, 'chan', 'space')
- volume_grad: float32 [96, 128, 64, 128], P(None, 'chan', 'space')
- filter_grad: float32 [27, 9216], replicated
- offset_grad: float32 [96], replicated
The draws below stay inside these ranges and needn't reach their ends.
All inputs are finite; a program needn't handle non-finite values.
Results may differ from the reference program's by a relative error of at most 0.0085.
Values may be sent and summed in bfloat16 or wider, within the bound.
A program may use at most 128 MiB of HBM per device.

```python
import math
import jax
import jax.numpy as jnp
from jax import lax

CIN = 96
COUT = 96
NZ = 128
NX = 128
NY = 64
CELLS = 1048576


def block_levels(key, extent, pieces, least, largest):
    level = 1.0
    for dim, parts in pieces:
        draws = jax.random.uniform(jax.random.fold_in(jax.random.fold_in(key, 6), dim), (parts,), jnp.float32, least / len(pieces), largest / len(pieces))
        level = level * jnp.repeat(jnp.exp(draws), extent[dim] // parts).reshape((-1,) + (1,) * (len(extent) - 1 - dim))
    return level


def centred(rng, extent, deviation, most, pieces=(), kind=jnp.bfloat16):
    entries = deviation * jax.random.normal(rng, extent, jnp.float32)
    if pieces:
        entries = entries * block_levels(rng, extent, pieces, -0.22, 0.18)
    return jnp.clip(entries, -most, most).astype(kind)


def setup_inputs(seed: int = 0) -> dict:
    keys = jax.random.split(jax.random.key(seed), 5)
    volume = centred(keys[0], (CIN, NX, NY, NZ), 1.0, 6.0, ((1, 64), (2, 4)), jnp.float32)
    filters = centred(keys[1], (27, CIN * COUT), (27 * CIN) ** -0.5, 0.125, (), jnp.float32)
    offsets = centred(keys[2], (COUT,), 0.5, 3.0, (), jnp.float32)
    upstream = centred(keys[3], (COUT, NX, NY, NZ), 1.0, 6.0, ((1, 64), (2, 4)), jnp.float32)
    return dict(volume=volume, filters=filters, offsets=offsets, upstream=upstream)


def convolve(field, kernel):
    return lax.conv_general_dilated(field[None], kernel, (1, 1, 1), 'SAME', dimension_numbers=('NCDHW', 'DHWIO', 'NCDHW'), precision=lax.Precision.HIGHEST)[0]

def reference(volume, filters, offsets, upstream):
    rounded = lax.optimization_barrier(volume.astype(jnp.bfloat16)).astype(jnp.float32)
    kernel = lax.optimization_barrier(filters.astype(jnp.bfloat16)).astype(jnp.float32)
    kernel = kernel.reshape(3, 3, 3, CIN, COUT)
    cotangent = lax.optimization_barrier(upstream.astype(jnp.bfloat16)).astype(jnp.float32)
    response_core, pullback = jax.vjp(convolve, rounded, kernel)
    response = response_core + offsets[:, None, None, None]
    volume_grad, kernel_grad = pullback(cotangent)
    factor = 1.0 / math.sqrt(CELLS)
    filter_grad = (kernel_grad * factor).reshape(27, CIN * COUT)
    offset_grad = lax.optimization_barrier(jnp.sum(cotangent, axis=(1, 2, 3))) * factor
    return (response, volume_grad, filter_grad, offset_grad)
```

```python
import functools
import math

import jax
import jax.numpy as jnp
from jax import lax
from jax.experimental import pallas as pl
from jax.experimental.pallas import tpu as pltpu
from jax.sharding import PartitionSpec as P

MESH = pl.DeviceIdType.MESH
C = 96
NXL = 2
NYL = 16
NZ = 128
GX, GY, GZ = 4, 4, 8
ROWS = 2048
HALF = ROWS // 2
PIECE = HALF // (GX * GY)
PART = PIECE // GZ
SIDES = [(dc, ds) for dc in (-1, 0, 1) for ds in (-1, 0, 1) if (dc, ds) != (0, 0)]
XY = [(dx, dy) for dx in (2, 1, 3, 0) for dy in (2, 1, 3, 0) if (dx, dy) != (0, 0)]


def body(factor, vol_hbm, up_hbm, wf_ref, wr_ref, off_ref, resp_ref, vgrad_ref, grads_ref,
         vbuf, ubuf, xs, cs, x3, acc, crecv, p2, xyrecv, zs, zrecv, zag, gath,
         load_sem, hsend, hrecv, csend, crsem, xysend, xyrsem, zsend, zrsem, gzsend, gzrsem,
         gxsend, gxrsem, fsend, frsem):
    chan = lax.axis_index("chan")
    space = lax.axis_index("space")
    nchan = 2 * GX * GY * 2
    nspace = GZ // 2
    core = lax.rem(chan, 2)
    cy = lax.rem(chan // 2, GY)
    cx = lax.rem(chan // (2 * GY), GX)
    zl = chan // (2 * GY * GX)
    cz = space * 2 + zl
    idx = cx * GY + cy

    def device(z, x, y, k):
        return {"chan": ((lax.rem(z, 2) * GX + x) * GY + y) * 2 + k, "space": z // 2}

    sibling = device(cz, cx, cy, 1 - core)
    neighbours = [
        {"chan": lax.rem(chan + dc + nchan, nchan), "space": lax.rem(space + ds + nspace, nspace)}
        for dc, ds in SIDES
    ]
    xy_peers = [(lax.rem(cx + dx, GX), lax.rem(cy + dy, GY)) for dx, dy in XY]
    z_peers = [lax.rem(cz + dz, GZ) for dz in range(1, GZ)]

    barrier = pltpu.get_barrier_semaphore()
    everyone = neighbours + [sibling]
    everyone += [device(cz, x, y, core) for x, y in xy_peers]
    everyone += [device(z, cx, cy, core) for z in z_peers]
    load_up = pltpu.make_async_copy(up_hbm, ubuf, load_sem.at[0])
    load_up.start()
    load_vol = pltpu.make_async_copy(vol_hbm, vbuf, load_sem.at[1])
    load_vol.start()
    for one in everyone:
        pl.semaphore_signal(barrier, inc=1, device_id=one, device_id_type=MESH)

    lane = lax.broadcasted_iota(jnp.int32, (C, NZ), 1)
    first, last = lane == 0, lane == NZ - 1

    load_up.wait()

    @pl.loop(0, NXL * NYL)
    def _(n):
        v = ubuf[pl.ds(n, C, stride=NXL * NYL), :]
        cs[n // NYL + 1, lax.rem(n, NYL) + 1] = v.astype(jnp.bfloat16)

    pl.semaphore_wait(barrier, len(everyone))

    def halo(field, which):
        copies = []
        for n, (dc, ds) in enumerate(SIDES):
            def span(d, width, far):
                if d == 0:
                    return pl.ds(1, width)
                if far:
                    return pl.ds(0 if d > 0 else width + 1, 1)
                return pl.ds(width if d > 0 else 1, 1)
            copies.append(pltpu.make_async_remote_copy(
                src_ref=field.at[span(dc, NXL, False), span(ds, NYL, False)],
                dst_ref=field.at[span(dc, NXL, True), span(ds, NYL, True)],
                send_sem=hsend.at[which, n],
                recv_sem=hrecv.at[which, n],
                device_id=neighbours[n],
                device_id_type=MESH,
            ))
        return copies

    def trim(field):
        @pl.when(chan == 0)
        def _():
            field[0] = jnp.zeros_like(field[0])

        @pl.when(chan == nchan - 1)
        def _():
            field[NXL + 1] = jnp.zeros_like(field[NXL + 1])

        @pl.when(space == 0)
        def _():
            field[:, 0] = jnp.zeros_like(field[:, 0])

        @pl.when(space == nspace - 1)
        def _():
            field[:, NYL + 1] = jnp.zeros_like(field[:, NYL + 1])

    cs_halo = halo(cs, 0)
    for copy in cs_halo:
        copy.start()

    load_vol.wait()

    @pl.loop(0, NXL * NYL)
    def _(n):
        i, j = n // NYL, lax.rem(n, NYL)
        v = vbuf[pl.ds(n, C, stride=NXL * NYL), :]
        rounded = v.astype(jnp.bfloat16)
        xs[i + 1, j + 1] = rounded
        x3[i, j, pl.ds(C, C)] = rounded
        x3[i, j, pl.ds(0, C)] = jnp.where(first, 0.0, pltpu.roll(v, 1, axis=1)).astype(jnp.bfloat16)
        x3[i, j, pl.ds(2 * C, C)] = jnp.where(last, 0.0, pltpu.roll(v, NZ - 1, axis=1)).astype(jnp.bfloat16)
        x3[i, j, pl.ds(3 * C, 16)] = jnp.ones((16, NZ), jnp.bfloat16)

    for copy in cs_halo:
        copy.wait_recv()
    trim(cs)
    xs_halo = halo(xs, 1)
    for copy in xs_halo:
        copy.start()

    acc[...] = jnp.zeros_like(acc)

    def window(field, i, j):
        return jnp.concatenate(
            [field[pl.ds(i, 3), pl.ds(j + k, 3)].reshape(9 * C, NZ) for k in range(2)], axis=1
        )

    @pl.loop(0, NXL * NYL // 2)
    def _(n):
        i, j = n // (NYL // 2), lax.rem(n, NYL // 2) * 2
        left = jnp.concatenate([x3[i, j], x3[i, j + 1]], axis=1)
        terms = lax.dot_general(
            left, window(cs, i, j), (((1,), (1,)), ((), ())), preferred_element_type=jnp.float32
        )
        terms = jnp.concatenate([terms, jnp.zeros((3 * C + 16, 32), jnp.float32)], axis=1)
        for t in range(7):
            acc[pl.ds(t * 3 * C, 3 * C)] += terms[: 3 * C, t * 128 : (t + 1) * 128]
        acc[pl.ds(7 * 3 * C, 16)] += terms[3 * C :, 384:512]

    def convolve(out, field, weights, toward, bias):
        def step(n):
            i, j = n // (NYL // 2), lax.rem(n, NYL // 2) * 2
            y = jnp.dot(weights[...], window(field, i, j), preferred_element_type=jnp.float32)
            for k in range(2):
                low, mid, high = (y[r * C : (r + 1) * C, k * NZ : (k + 1) * NZ] for r in toward)
                total = mid + jnp.where(first, 0.0, pltpu.roll(low, 1, axis=1))
                total = total + jnp.where(last, 0.0, pltpu.roll(high, NZ - 1, axis=1))
                if bias is not None:
                    total = total + bias
                out[pl.ds(i * NYL + j + k, C, stride=NXL * NYL), :] = total
        return step

    square = lax.broadcasted_iota(jnp.int32, (C, C), 0) == lax.broadcasted_iota(jnp.int32, (C, C), 1)
    bias = jnp.sum(jnp.where(square, off_ref[...], 0.0), axis=1, keepdims=True)
    data_step = convolve(vgrad_ref, cs, wr_ref, (2, 1, 0), None)
    forward_step = convolve(resp_ref, xs, wf_ref, (0, 1, 2), bias)

    to_sibling = pltpu.make_async_remote_copy(
        src_ref=acc.at[pl.ds(pl.multiple_of((1 - core) * HALF, HALF), HALF)],
        dst_ref=crecv, send_sem=csend, recv_sem=crsem, device_id=sibling, device_id_type=MESH,
    )
    to_sibling.start()
    pl.loop(0, 6)(data_step)
    to_sibling.wait_recv()

    @pl.loop(0, GX * GY)
    def _(n):
        at = pl.multiple_of(core * HALF + n * PIECE, PIECE)
        total = acc[pl.ds(at, PIECE)] + crecv[pl.ds(pl.multiple_of(n * PIECE, PIECE), PIECE)]
        p2[n] = total.astype(jnp.bfloat16)

    mine = pl.multiple_of(core * HALF + idx * PIECE, PIECE)
    zs[...] = acc[pl.ds(mine, PIECE)] + crecv[pl.ds(pl.multiple_of(idx * PIECE, PIECE), PIECE)]

    xy_copies = []
    for n, (x, y) in enumerate(xy_peers):
        copy = pltpu.make_async_remote_copy(
            src_ref=p2.at[x * GY + y], dst_ref=xyrecv.at[n],
            send_sem=xysend.at[n], recv_sem=xyrsem.at[n],
            device_id=device(cz, x, y, core), device_id_type=MESH,
        )
        copy.start()
        xy_copies.append(copy)
    pl.loop(6, 16)(data_step)
    for n, copy in enumerate(xy_copies):
        copy.wait_recv()
    total = zs[...]
    for n in range(len(XY)):
        total = total + xyrecv[n].astype(jnp.float32)
    zs[...] = total

    z_copies = []
    for n, z in enumerate(z_peers):
        copy = pltpu.make_async_remote_copy(
            src_ref=zs.at[pl.ds(pl.multiple_of(z * PART, PART), PART)], dst_ref=zrecv.at[n],
            send_sem=zsend.at[n], recv_sem=zrsem.at[n],
            device_id=device(z, cx, cy, core), device_id_type=MESH,
        )
        copy.start()
        z_copies.append(copy)
    for copy in xs_halo:
        copy.wait_recv()
    trim(xs)
    pl.loop(0, 4)(forward_step)
    for copy in z_copies:
        copy.wait_recv()
    here = pl.ds(pl.multiple_of(cz * PART, PART), PART)
    total = zs[here]
    for n in range(len(z_peers)):
        total = total + zrecv[n]
    zag[here] = total * factor

    gz_copies = []
    for n, z in enumerate(z_peers):
        copy = pltpu.make_async_remote_copy(
            src_ref=zag.at[here], dst_ref=zag.at[here],
            send_sem=gzsend.at[n], recv_sem=gzrsem.at[n],
            device_id=device(z, cx, cy, core), device_id_type=MESH,
        )
        copy.start()
        gz_copies.append(copy)
    pl.loop(4, 8)(forward_step)
    for copy in gz_copies:
        copy.wait_recv()
    gath[core, idx] = zag[...].astype(jnp.bfloat16)

    gx_copies = []
    for n, (x, y) in enumerate(xy_peers):
        copy = pltpu.make_async_remote_copy(
            src_ref=gath.at[core, idx], dst_ref=gath.at[core, idx],
            send_sem=gxsend.at[n], recv_sem=gxrsem.at[n],
            device_id=device(cz, x, y, core), device_id_type=MESH,
        )
        copy.start()
        gx_copies.append(copy)

    def hand_on(n, source):
        return pltpu.make_async_remote_copy(
            src_ref=gath.at[core, source], dst_ref=gath.at[core, source],
            send_sem=fsend.at[n], recv_sem=frsem.at[n], device_id=sibling, device_id_type=MESH,
        )

    forwards = [hand_on(len(XY), idx)]
    forwards[0].start()
    pl.loop(8, 16)(forward_step)
    for n, (dx, dy) in enumerate(XY):
        gx_copies[n].wait_recv()
        source = lax.rem(cx - dx + GX, GX) * GY + lax.rem(cy - dy + GY, GY)
        forwards.append(hand_on(n, source))
        forwards[-1].start()
    for copy in forwards:
        copy.wait_recv()

    @pl.loop(0, GX * GY)
    def _(n):
        for k in range(2):
            grads_ref[pl.ds(pl.multiple_of(k * HALF + n * PIECE, PIECE), PIECE)] = gath[k, n].astype(jnp.float32)

    for copy in cs_halo + xs_halo + [to_sibling] + xy_copies + z_copies + gz_copies + gx_copies + forwards:
        copy.wait_send()


def on_device(volume, filters, offsets, upstream):
    cells = CELLS = volume.shape[1] * volume.shape[2] * volume.shape[3]
    cells = CELLS * lax.axis_size("chan") * lax.axis_size("space")
    factor = 1.0 / math.sqrt(cells)
    kernel = filters.astype(jnp.bfloat16).reshape(3, 3, 3, C, C)
    wf = jnp.transpose(kernel, (2, 4, 0, 1, 3)).reshape(3 * C, 9 * C)
    wr = jnp.transpose(kernel[::-1, ::-1], (2, 3, 0, 1, 4)).reshape(3 * C, 9 * C)
    flat = (C * NXL * NYL, NZ)
    f32, bf16 = jnp.float32, jnp.bfloat16
    vmem = pl.BlockSpec(memory_space=pltpu.VMEM)
    hbm = pl.BlockSpec(memory_space=pl.ANY)
    dma = pltpu.SemaphoreType.DMA
    resp, vgrad, grads = pl.pallas_call(
        functools.partial(body, factor),
        out_shape=[
            jax.ShapeDtypeStruct(flat, f32),
            jax.ShapeDtypeStruct(flat, f32),
            jax.ShapeDtypeStruct((ROWS, 128), f32),
        ],
        in_specs=[hbm, hbm, vmem, vmem, vmem],
        out_specs=[vmem, vmem, vmem],
        scratch_shapes=[
            pltpu.VMEM(flat, f32),
            pltpu.VMEM(flat, f32),
            pltpu.VMEM((NXL + 2, NYL + 2, C, NZ), bf16),
            pltpu.VMEM((NXL + 2, NYL + 2, C, NZ), bf16),
            pltpu.VMEM((NXL, NYL, 3 * C + 16, NZ), bf16),
            pltpu.VMEM((ROWS, 128), f32),
            pltpu.VMEM((HALF, 128), f32),
            pltpu.VMEM((GX * GY, PIECE, 128), bf16),
            pltpu.VMEM((GX * GY - 1, PIECE, 128), bf16),
            pltpu.VMEM((PIECE, 128), f32),
            pltpu.VMEM((GZ - 1, PART, 128), f32),
            pltpu.VMEM((PIECE, 128), f32),
            pltpu.VMEM((2, GX * GY, PIECE, 128), bf16),
            dma((2,)),
            dma((2, 8)),
            dma((2, 8)),
            dma,
            dma,
            dma((GX * GY - 1,)),
            dma((GX * GY - 1,)),
            dma((GZ - 1,)),
            dma((GZ - 1,)),
            dma((GZ - 1,)),
            dma((GZ - 1,)),
            dma((GX * GY - 1,)),
            dma((GX * GY - 1,)),
            dma((GX * GY,)),
            dma((GX * GY,)),
        ],
        compiler_params=pltpu.CompilerParams(
            collective_id=0, has_side_effects=True, vmem_limit_bytes=48 * 1024 * 1024
        ),
    )(volume.reshape(flat), upstream.reshape(flat), wf, wr, offsets.reshape(1, C))
    columns = jnp.concatenate([grads[t * 3 * C : (t + 1) * 3 * C] for t in range(7)], axis=1)[:, : 9 * C]
    taps = columns.reshape(3, C, 3, 3, C)[:, :, ::-1, ::-1]
    filter_grad = jnp.transpose(taps, (2, 3, 0, 1, 4)).reshape(27, C * C)
    offset_grad = grads[7 * 3 * C, :C]
    return (resp.reshape(volume.shape), vgrad.reshape(volume.shape), filter_grad, offset_grad)


def solution(mesh):
    placed = (P(None, "chan", "space", None), P(), P(), P(None, "chan", "space", None))
    return jax.shard_map(
        on_device,
        mesh=mesh,
        in_specs=placed,
        out_specs=(P(None, "chan", "space", None), P(None, "chan", "space", None), P(), P()),
        check_vma=False,
    )
```

```python
import functools
import math

import jax
import jax.numpy as jnp
from jax import lax
from jax.experimental import pallas as pl
from jax.experimental.pallas import tpu as pltpu
from jax.sharding import PartitionSpec as P

MESH = pl.DeviceIdType.MESH
C = 96
NXL = 2
NYL = 16
NZ = 128
GX, GY, GZ = 4, 4, 8
ROWS = 2048
HALF = ROWS // 2
PIECE = HALF // (GX * GY)
PART = PIECE // GZ
SIDES = [(dc, ds) for dc in (-1, 0, 1) for ds in (-1, 0, 1) if (dc, ds) != (0, 0)]
XY = [(dx, dy) for dx in (2, 1, 3, 0) for dy in (2, 1, 3, 0) if (dx, dy) != (0, 0)]


def body(factor, vol_hbm, up_hbm, fbuf, off_ref, resp_ref, vgrad_ref, grads_ref,
         vbuf, ubuf, fs, wf_ref, wr_ref, xs, cs, x3, acc, crecv, p2, xyrecv, zs, zrecv, zag, gath,
         load_sem, hsend, hrecv, csend, crsem, xysend, xyrsem, zsend, zrsem, gzsend, gzrsem,
         gxsend, gxrsem, fsend, frsem):
    chan = lax.axis_index("chan")
    space = lax.axis_index("space")
    nchan = 2 * GX * GY * 2
    nspace = GZ // 2
    core = lax.rem(chan, 2)
    cy = lax.rem(chan // 2, GY)
    cx = lax.rem(chan // (2 * GY), GX)
    zl = chan // (2 * GY * GX)
    cz = space * 2 + zl
    idx = cx * GY + cy

    def device(z, x, y, k):
        return {"chan": ((lax.rem(z, 2) * GX + x) * GY + y) * 2 + k, "space": z // 2}

    sibling = device(cz, cx, cy, 1 - core)
    neighbours = [
        {"chan": lax.rem(chan + dc + nchan, nchan), "space": lax.rem(space + ds + nspace, nspace)}
        for dc, ds in SIDES
    ]
    xy_peers = [(lax.rem(cx + dx, GX), lax.rem(cy + dy, GY)) for dx, dy in XY]
    z_peers = [lax.rem(cz + dz, GZ) for dz in range(1, GZ)]

    barrier = pltpu.get_barrier_semaphore()
    everyone = neighbours + [sibling]
    everyone += [device(cz, x, y, core) for x, y in xy_peers]
    everyone += [device(z, cx, cy, core) for z in z_peers]
    load_up = pltpu.make_async_copy(up_hbm, ubuf, load_sem.at[0])
    load_up.start()
    load_vol = pltpu.make_async_copy(vol_hbm, vbuf, load_sem.at[1])
    load_vol.start()
    for one in everyone:
        pl.semaphore_signal(barrier, inc=1, device_id=one, device_id_type=MESH)

    lane = lax.broadcasted_iota(jnp.int32, (C, NZ), 1)
    first, last = lane == 0, lane == NZ - 1

    load_up.wait()

    @pl.loop(0, NXL * NYL)
    def _(n):
        v = ubuf[pl.ds(n, C, stride=NXL * NYL), :]
        cs[n // NYL + 1, lax.rem(n, NYL) + 1] = v.astype(jnp.bfloat16)

    pl.semaphore_wait(barrier, len(everyone))

    def halo(field, which):
        copies = []
        for n, (dc, ds) in enumerate(SIDES):
            def span(d, width, far):
                if d == 0:
                    return pl.ds(1, width)
                if far:
                    return pl.ds(0 if d > 0 else width + 1, 1)
                return pl.ds(width if d > 0 else 1, 1)
            copies.append(pltpu.make_async_remote_copy(
                src_ref=field.at[span(dc, NXL, False), span(ds, NYL, False)],
                dst_ref=field.at[span(dc, NXL, True), span(ds, NYL, True)],
                send_sem=hsend.at[which, n],
                recv_sem=hrecv.at[which, n],
                device_id=neighbours[n],
                device_id_type=MESH,
            ))
        return copies

    def trim(field):
        @pl.when(chan == 0)
        def _():
            field[0] = jnp.zeros_like(field[0])

        @pl.when(chan == nchan - 1)
        def _():
            field[NXL + 1] = jnp.zeros_like(field[NXL + 1])

        @pl.when(space == 0)
        def _():
            field[:, 0] = jnp.zeros_like(field[:, 0])

        @pl.when(space == nspace - 1)
        def _():
            field[:, NYL + 1] = jnp.zeros_like(field[:, NYL + 1])

    cs_halo = halo(cs, 0)
    for copy in cs_halo:
        copy.start()

    load_vol.wait()

    @pl.loop(0, NXL * NYL)
    def _(n):
        i, j = n // NYL, lax.rem(n, NYL)
        v = vbuf[pl.ds(n, C, stride=NXL * NYL), :]
        rounded = v.astype(jnp.bfloat16)
        xs[i + 1, j + 1] = rounded
        x3[i, j, pl.ds(C, C)] = rounded
        x3[i, j, pl.ds(0, C)] = jnp.where(first, 0.0, pltpu.roll(v, 1, axis=1)).astype(jnp.bfloat16)
        x3[i, j, pl.ds(2 * C, C)] = jnp.where(last, 0.0, pltpu.roll(v, NZ - 1, axis=1)).astype(jnp.bfloat16)
        x3[i, j, pl.ds(3 * C, 16)] = jnp.ones((16, NZ), jnp.bfloat16)


    @pl.loop(0, C // 4)
    def _(n):
        v = fbuf[:, pl.ds(pl.multiple_of(n * 4 * C, 128), 4 * C)]
        for k in range(4):
            fs[pl.ds(pl.multiple_of((n * 4 + k) * 32, 32), 27), :C] = v[:, k * C : (k + 1) * C]

    for r in range(3):
        taps = [fs[pl.ds(3 * n + r, C, stride=32), :][:, :C] for n in range(9)]
        wr_ref[pl.ds(r * C, C), :] = jnp.concatenate(taps, axis=1).astype(jnp.bfloat16)
        wf_ref[pl.ds(r * C, C), :] = jnp.concatenate([tap.T for tap in taps], axis=1).astype(jnp.bfloat16)

    for copy in cs_halo:
        copy.wait_recv()
    trim(cs)
    xs_halo = halo(xs, 1)
    for copy in xs_halo:
        copy.start()

    acc[...] = jnp.zeros_like(acc)

    def window(field, i, j, order):
        return jnp.concatenate(
            [
                jnp.concatenate([field[i + p, j + k + q] for p in order for q in order], axis=0)
                for k in range(2)
            ],
            axis=1,
        )

    @pl.loop(0, NXL * NYL // 2)
    def _(n):
        i, j = n // (NYL // 2), lax.rem(n, NYL // 2) * 2
        left = jnp.concatenate([x3[i, j], x3[i, j + 1]], axis=1)
        terms = lax.dot_general(
            left, window(cs, i, j, (2, 1, 0)), (((1,), (1,)), ((), ())), preferred_element_type=jnp.float32
        )
        terms = jnp.concatenate([terms, jnp.zeros((3 * C + 16, 32), jnp.float32)], axis=1)
        for t in range(7):
            acc[pl.ds(t * 3 * C, 3 * C)] += terms[: 3 * C, t * 128 : (t + 1) * 128]
        acc[pl.ds(7 * 3 * C, 16)] += terms[3 * C :, 384:512]

    def convolve(out, field, weights, toward, bias):
        order = toward

        def step(n):
            i, j = n // (NYL // 2), lax.rem(n, NYL // 2) * 2
            y = jnp.dot(weights[...], window(field, i, j, order), preferred_element_type=jnp.float32)
            for k in range(2):
                low, mid, high = (y[r * C : (r + 1) * C, k * NZ : (k + 1) * NZ] for r in toward)
                total = mid + jnp.where(first, 0.0, pltpu.roll(low, 1, axis=1))
                total = total + jnp.where(last, 0.0, pltpu.roll(high, NZ - 1, axis=1))
                if bias is not None:
                    total = total + bias
                out[pl.ds(i * NYL + j + k, C, stride=NXL * NYL), :] = total
        return step

    square = lax.broadcasted_iota(jnp.int32, (C, C), 0) == lax.broadcasted_iota(jnp.int32, (C, C), 1)
    bias = jnp.sum(jnp.where(square, off_ref[...], 0.0), axis=1, keepdims=True)
    data_step = convolve(vgrad_ref, cs, wr_ref, (2, 1, 0), None)
    forward_step = convolve(resp_ref, xs, wf_ref, (0, 1, 2), bias)

    to_sibling = pltpu.make_async_remote_copy(
        src_ref=acc.at[pl.ds(pl.multiple_of((1 - core) * HALF, HALF), HALF)],
        dst_ref=crecv, send_sem=csend, recv_sem=crsem, device_id=sibling, device_id_type=MESH,
    )
    to_sibling.start()
    pl.loop(0, 6)(data_step)
    to_sibling.wait_recv()

    @pl.loop(0, GX * GY)
    def _(n):
        at = pl.multiple_of(core * HALF + n * PIECE, PIECE)
        total = acc[pl.ds(at, PIECE)] + crecv[pl.ds(pl.multiple_of(n * PIECE, PIECE), PIECE)]
        p2[n] = total.astype(jnp.bfloat16)

    mine = pl.multiple_of(core * HALF + idx * PIECE, PIECE)
    zs[...] = acc[pl.ds(mine, PIECE)] + crecv[pl.ds(pl.multiple_of(idx * PIECE, PIECE), PIECE)]

    xy_copies = []
    for n, (x, y) in enumerate(xy_peers):
        copy = pltpu.make_async_remote_copy(
            src_ref=p2.at[x * GY + y], dst_ref=xyrecv.at[n],
            send_sem=xysend.at[n], recv_sem=xyrsem.at[n],
            device_id=device(cz, x, y, core), device_id_type=MESH,
        )
        copy.start()
        xy_copies.append(copy)
    pl.loop(6, 16)(data_step)
    for n, copy in enumerate(xy_copies):
        copy.wait_recv()
    total = zs[...]
    for n in range(len(XY)):
        total = total + xyrecv[n].astype(jnp.float32)
    zs[...] = total

    z_copies = []
    for n, z in enumerate(z_peers):
        copy = pltpu.make_async_remote_copy(
            src_ref=zs.at[pl.ds(pl.multiple_of(z * PART, PART), PART)], dst_ref=zrecv.at[n],
            send_sem=zsend.at[n], recv_sem=zrsem.at[n],
            device_id=device(z, cx, cy, core), device_id_type=MESH,
        )
        copy.start()
        z_copies.append(copy)
    for copy in xs_halo:
        copy.wait_recv()
    trim(xs)
    pl.loop(0, 4)(forward_step)
    for copy in z_copies:
        copy.wait_recv()
    here = pl.ds(pl.multiple_of(cz * PART, PART), PART)
    total = zs[here]
    for n in range(len(z_peers)):
        total = total + zrecv[n]
    zag[here] = total * factor

    gz_copies = []
    for n, z in enumerate(z_peers):
        copy = pltpu.make_async_remote_copy(
            src_ref=zag.at[here], dst_ref=zag.at[here],
            send_sem=gzsend.at[n], recv_sem=gzrsem.at[n],
            device_id=device(z, cx, cy, core), device_id_type=MESH,
        )
        copy.start()
        gz_copies.append(copy)
    pl.loop(4, 8)(forward_step)
    for copy in gz_copies:
        copy.wait_recv()
    gath[core, idx] = zag[...].astype(jnp.bfloat16)

    gx_copies = []
    for n, (x, y) in enumerate(xy_peers):
        copy = pltpu.make_async_remote_copy(
            src_ref=gath.at[core, idx], dst_ref=gath.at[core, idx],
            send_sem=gxsend.at[n], recv_sem=gxrsem.at[n],
            device_id=device(cz, x, y, core), device_id_type=MESH,
        )
        copy.start()
        gx_copies.append(copy)

    def hand_on(n, source):
        return pltpu.make_async_remote_copy(
            src_ref=gath.at[core, source], dst_ref=gath.at[core, source],
            send_sem=fsend.at[n], recv_sem=frsem.at[n], device_id=sibling, device_id_type=MESH,
        )

    forwards = [hand_on(len(XY), idx)]
    forwards[0].start()
    pl.loop(8, 16)(forward_step)
    for n, (dx, dy) in enumerate(XY):
        gx_copies[n].wait_recv()
        source = lax.rem(cx - dx + GX, GX) * GY + lax.rem(cy - dy + GY, GY)
        forwards.append(hand_on(n, source))
        forwards[-1].start()
    for copy in forwards:
        copy.wait_recv()

    @pl.loop(0, GX * GY)
    def _(n):
        for k in range(2):
            grads_ref[pl.ds(pl.multiple_of(k * HALF + n * PIECE, PIECE), PIECE)] = gath[k, n].astype(jnp.float32)

    for copy in cs_halo + xs_halo + [to_sibling] + xy_copies + z_copies + gz_copies + gx_copies + forwards:
        copy.wait_send()


def finish(resp_ref, vgrad_ref, grads_ref, resp_hbm, vgrad_hbm, filt_hbm, bias_ref, fs, fout, sem):
    copies = [
        pltpu.make_async_copy(resp_ref, resp_hbm, sem.at[0]),
        pltpu.make_async_copy(vgrad_ref, vgrad_hbm, sem.at[1]),
    ]
    for copy in copies:
        copy.start()
    bias_ref[...] = grads_ref[pl.ds(7 * 3 * C, 1), :]
    for r in range(3):
        tiles = [grads_ref[pl.ds(t * 3 * C + r * C, C), :] for t in range(7)]
        columns = jnp.concatenate(tiles, axis=1)
        for n in range(9):
            fs[pl.ds(3 * n + r, C, stride=32), :] = jnp.concatenate(
                [columns[:, n * C : (n + 1) * C], jnp.zeros((C, 32), jnp.float32)], axis=1
            )

    @pl.loop(0, C // 4)
    def _(n):
        parts = [fs[pl.ds(pl.multiple_of((n * 4 + k) * 32, 32), 27), :][:, :C] for k in range(4)]
        fout[:, pl.ds(pl.multiple_of(n * 4 * C, 128), 4 * C)] = jnp.concatenate(parts, axis=1)

    last = pltpu.make_async_copy(fout, filt_hbm, sem.at[2])
    last.start()
    for copy in copies + [last]:
        copy.wait()


def on_device(volume, filters, offsets, upstream):
    cells = volume.shape[1] * volume.shape[2] * volume.shape[3]
    cells = cells * lax.axis_size("chan") * lax.axis_size("space")
    factor = 1.0 / math.sqrt(cells)
    flat = (C * NXL * NYL, NZ)
    f32, bf16 = jnp.float32, jnp.bfloat16
    vmem = pl.BlockSpec(memory_space=pltpu.VMEM)
    hbm = pl.BlockSpec(memory_space=pl.ANY)
    dma = pltpu.SemaphoreType.DMA
    resp, vgrad, grads = pl.pallas_call(
        functools.partial(body, factor),
        out_shape=[
            jax.ShapeDtypeStruct(flat, f32),
            jax.ShapeDtypeStruct(flat, f32),
            jax.ShapeDtypeStruct((ROWS, 128), f32),
        ],
        in_specs=[hbm, hbm, vmem, vmem],
        out_specs=[vmem, vmem, vmem],
        scratch_shapes=[
            pltpu.VMEM(flat, f32),
            pltpu.VMEM(flat, f32),
            pltpu.VMEM((C * 32, 128), f32),
            pltpu.VMEM((3 * C, 9 * C), bf16),
            pltpu.VMEM((3 * C, 9 * C), bf16),
            pltpu.VMEM((NXL + 2, NYL + 2, C, NZ), bf16),
            pltpu.VMEM((NXL + 2, NYL + 2, C, NZ), bf16),
            pltpu.VMEM((NXL, NYL, 3 * C + 16, NZ), bf16),
            pltpu.VMEM((ROWS, 128), f32),
            pltpu.VMEM((HALF, 128), f32),
            pltpu.VMEM((GX * GY, PIECE, 128), bf16),
            pltpu.VMEM((GX * GY - 1, PIECE, 128), bf16),
            pltpu.VMEM((PIECE, 128), f32),
            pltpu.VMEM((GZ - 1, PART, 128), f32),
            pltpu.VMEM((PIECE, 128), f32),
            pltpu.VMEM((2, GX * GY, PIECE, 128), bf16),
            dma((2,)),
            dma((2, 8)),
            dma((2, 8)),
            dma,
            dma,
            dma((GX * GY - 1,)),
            dma((GX * GY - 1,)),
            dma((GZ - 1,)),
            dma((GZ - 1,)),
            dma((GZ - 1,)),
            dma((GZ - 1,)),
            dma((GX * GY - 1,)),
            dma((GX * GY - 1,)),
            dma((GX * GY,)),
            dma((GX * GY,)),
        ],
        compiler_params=pltpu.CompilerParams(
            collective_id=0, has_side_effects=True, vmem_limit_bytes=48 * 1024 * 1024
        ),
    )(volume.reshape(flat), upstream.reshape(flat), filters, offsets.reshape(1, C))
    resp, vgrad, filter_grad, offset_grad = pl.pallas_call(
        finish,
        out_shape=[
            jax.ShapeDtypeStruct(flat, f32),
            jax.ShapeDtypeStruct(flat, f32),
            jax.ShapeDtypeStruct((27, C * C), f32),
            jax.ShapeDtypeStruct((1, 128), f32),
        ],
        in_specs=[vmem, vmem, vmem],
        out_specs=[hbm, hbm, hbm, vmem],
        scratch_shapes=[pltpu.VMEM((C * 32, 128), f32), pltpu.VMEM((27, C * C), f32), dma((3,))],
        compiler_params=pltpu.CompilerParams(vmem_limit_bytes=16 * 1024 * 1024),
    )(resp, vgrad, grads)
    return (resp.reshape(volume.shape), vgrad.reshape(volume.shape), filter_grad, offset_grad[0, :C])


def solution(mesh):
    placed = (P(None, "chan", "space", None), P(), P(), P(None, "chan", "space", None))
    return jax.shard_map(
        on_device,
        mesh=mesh,
        in_specs=placed,
        out_specs=(P(None, "chan", "space", None), P(None, "chan", "space", None), P(), P()),
        check_vma=False,
    )
```

```python
import functools
import math

import jax
import jax.numpy as jnp
from jax import lax
from jax.experimental import pallas as pl
from jax.experimental.pallas import tpu as pltpu
from jax.sharding import PartitionSpec as P

MESH = pl.DeviceIdType.MESH
C = 96
NXL = 2
NYL = 16
NZ = 128
GX, GY, GZ = 4, 4, 8
TALL = 3 * C
ROWS = 2048
HALF = ROWS // 2
PIECE = HALF // (GX * GY)
BIAS = 7 * TALL
QS = (1, 0, 2)
HALVES = ((1, 9), (10, 7))
XY = [(dx, dy) for dx in (2, 1, 3, 0) for dy in (2, 1, 3, 0) if (dx, dy) != (0, 0)]
NT = (((1,), (1,)), ((), ()))


def body(factor, vol_hbm, up_hbm, filt_hbm, off_ref, resp0, resp1, vgrad0, vgrad1, gath,
         vbuf, ubuf, fbuf, fs, wf_ref, wr_ref, xs, cs, x3, acc, crecv, p2, xyrecv, own, zall,
         load_sem, hsend, hrecv, csend, crsem, xysend, xyrsem, zsend, zrsem,
         gxsend, gxrsem, fsend, frsem):
    f32, bf16 = jnp.float32, jnp.bfloat16
    chan = lax.axis_index("chan")
    space = lax.axis_index("space")
    nchan = 4 * GX * GY
    nspace = GZ // 2
    core = lax.rem(chan, 2)
    cy = lax.rem(chan // 2, GY)
    cx = lax.rem(chan // (2 * GY), GX)
    zl = chan // (2 * GY * GX)
    cz = space * 2 + zl
    idx = cx * GY + cy

    def device(z, x, y, k):
        return {"chan": ((lax.rem(z, 2) * GX + x) * GY + y) * 2 + k, "space": z // 2}

    def beside(dc, ds):
        return {"chan": lax.rem(chan + dc + nchan, nchan), "space": lax.rem(space + ds + nspace, nspace)}

    sibling = device(cz, cx, cy, 1 - core)
    xy_peers = [(lax.rem(cx + dx, GX), lax.rem(cy + dy, GY)) for dx, dy in XY]
    z_peers = [lax.rem(cz + dz, GZ) for dz in (4, 3, 5, 2, 6, 1, 7)]

    barrier = pltpu.get_barrier_semaphore()
    everyone = [beside(dc, ds) for dc in (-1, 1, 0) for ds in (-1, 1, 0) if (dc, ds) != (0, 0)]
    everyone += [sibling]
    everyone += [device(cz, x, y, core) for x, y in xy_peers]
    everyone += [device(z, cx, cy, core) for z in z_peers]
    load_up = pltpu.make_async_copy(up_hbm, ubuf, load_sem.at[0])
    load_up.start()
    for one in everyone:
        pl.semaphore_signal(barrier, inc=1, device_id=one, device_id_type=MESH)
    load_vol = pltpu.make_async_copy(vol_hbm, vbuf, load_sem.at[1])
    load_vol.start()
    load_filt = pltpu.make_async_copy(filt_hbm, fbuf, load_sem.at[2])
    load_filt.start()

    for field in (cs, xs):
        @pl.when(chan == 0)
        def _():
            field[0] = jnp.zeros((NYL + 2, C, NZ), bf16)

        @pl.when(chan == nchan - 1)
        def _():
            field[NXL + 1] = jnp.zeros((NYL + 2, C, NZ), bf16)

        @pl.when(space == 0)
        def _():
            for n in range(NXL + 2):
                field[n, 0] = jnp.zeros((C, NZ), bf16)

        @pl.when(space == nspace - 1)
        def _():
            for n in range(NXL + 2):
                field[n, NYL + 1] = jnp.zeros((C, NZ), bf16)

    lane = lax.broadcasted_iota(jnp.int32, (C, NZ), 1)
    first, last = lane == 0, lane == NZ - 1

    load_up.wait()

    @pl.loop(0, NXL * NYL, unroll=4)
    def _(n):
        v = ubuf[pl.ds(n, C, stride=NXL * NYL), :]
        cs[n // NYL + 1, lax.rem(n, NYL) + 1] = v.astype(bf16)

    pl.semaphore_wait(barrier, len(everyone))
    pending = []

    def inside(dc, ds):
        ok = None
        for d, at, count in ((dc, chan, nchan), (ds, space, nspace)):
            if d != 0:
                here = at < count - 1 if d > 0 else at > 0
                ok = here if ok is None else jnp.logical_and(ok, here)
        return ok

    class Halo:
        def __init__(self, field, which, n, dc, ds, row, count):
            plane_from, plane_to, planes = {-1: (1, NXL + 1, 1), 0: (1, 1, NXL), 1: (NXL, 0, 1)}[dc]
            row_from, row_to = {-1: (1, NYL + 1), 0: (row, row), 1: (NYL, 0)}[ds]
            self.copy = pltpu.make_async_remote_copy(
                src_ref=field.at[pl.ds(plane_from, planes), pl.ds(row_from, count)],
                dst_ref=field.at[pl.ds(plane_to, planes), pl.ds(row_to, count)],
                send_sem=hsend.at[which, n], recv_sem=hrecv.at[which, n],
                device_id=beside(dc, ds), device_id_type=MESH,
            )
            self.to, self.source = inside(dc, ds), inside(-dc, -ds)

        def start(self):
            pl.when(self.to)(self.copy.start)

        def wait_recv(self):
            pl.when(self.source)(self.copy.wait_recv)

        def wait_send(self):
            pl.when(self.to)(self.copy.wait_send)

    def halo(field, which):
        sides = [(dc, ds, 0, 1) for ds in (-1, 1) for dc in (0,)]
        sides += [(dc, ds, 0, 1) for dc in (-1, 1) for ds in (-1, 1)]
        sides += [(dc, 0, row, count) for row, count in HALVES for dc in (-1, 1)]
        return [Halo(field, which, n, *side) for n, side in enumerate(sides)]

    cs_halo = halo(cs, 0)
    for copy in cs_halo:
        copy.start()
    pending += cs_halo

    load_vol.wait()

    @pl.loop(0, NXL * NYL, unroll=4)
    def _(n):
        i, j = n // NYL, lax.rem(n, NYL)
        v = vbuf[pl.ds(n, C, stride=NXL * NYL), :]
        rounded = v.astype(bf16)
        xs[i + 1, j + 1] = rounded
        x3[i, j, pl.ds(C, C)] = rounded
        x3[i, j, pl.ds(0, C)] = jnp.where(first, 0.0, pltpu.roll(v, 1, axis=1)).astype(bf16)
        x3[i, j, pl.ds(2 * C, C)] = jnp.where(last, 0.0, pltpu.roll(v, NZ - 1, axis=1)).astype(bf16)
        x3[i, j, pl.ds(TALL, 16)] = jnp.ones((16, NZ), bf16)

    acc[pl.ds(6 * TALL, TALL)] = jnp.zeros((TALL, 128), f32)
    acc[pl.ds(BIAS, 32)] = jnp.zeros((32, 128), f32)
    step = NYL // 2

    def shifted(i, j):
        return jnp.concatenate([x3[i, j + k] for k in range(step)], axis=1)

    def terms(i, j, p, fresh):
        def rows(k):
            return jnp.concatenate([cs[i + 2 - p, j + k + 2 - q] for q in QS], axis=0)[:256]

        right = jnp.concatenate([rows(k) for k in range(step)], axis=1)
        v = lax.dot_general(shifted(i, j), right, NT, preferred_element_type=f32)
        for t in range(2):
            at = pl.ds((2 * p + t) * TALL, TALL)
            part = v[:TALL, t * 128 : (t + 1) * 128]
            acc[at] = part if fresh else acc[at] + part
        if p == 1:
            acc[pl.ds(BIAS, 16)] += v[TALL:, :128]

    def rest(i, j):
        def rows(k):
            return jnp.concatenate([cs[i + 2 - p, j + k + 2 - QS[2]][C - 32 :] for p in range(3)], axis=0)

        right = jnp.concatenate([rows(k) for k in range(step)], axis=1)
        v = lax.dot_general(shifted(i, j), right, NT, preferred_element_type=f32)
        acc[pl.ds(6 * TALL, TALL), : 3 * 32] += v[:TALL]

    rows_halo, corner_halo, plane_halo = cs_halo[:2], cs_halo[2:6], cs_halo[6:]
    for copy in rows_halo:
        copy.wait_recv()
    for j in (0, step):
        terms(0, j, 0, j == 0)
        terms(0, j, 1, j == 0)
        terms(1, j, 1, False)
        terms(1, j, 2, j == 0)

    load_filt.wait()

    for n in range(C // 4):
        v = fbuf[:, n * 4 * C : (n + 1) * 4 * C]
        for k in range(4):
            fs[pl.ds((n * 4 + k) * 32, 27), :C] = v[:, k * C : (k + 1) * C]
    for r in range(3):
        taps = [fs[pl.ds(3 * n + r, C, stride=32), :][:, :C] for n in range(9)]
        wr_ref[pl.ds(r * C, C), :] = jnp.concatenate(taps, axis=1).astype(bf16)
        wf_ref[pl.ds(r * C, C), :] = jnp.concatenate([tap.T for tap in taps], axis=1).astype(bf16)

    for copy in corner_halo + plane_halo[:2]:
        copy.wait_recv()
    xs_halo = halo(xs, 1)
    for part in range(2):
        if part == 1:
            for copy in plane_halo[2:]:
                copy.wait_recv()
            for copy in xs_halo:
                copy.start()
            pending += xs_halo
        j = part * step
        terms(0, j, 2, False)
        terms(1, j, 0, False)
        rest(0, j)
        rest(1, j)

    order = [x * GY + y for x, y in xy_peers] + [idx]
    core_copies = []
    for n, piece in enumerate(order):
        copy = pltpu.make_async_remote_copy(
            src_ref=acc.at[pl.ds(pl.multiple_of((1 - core) * HALF + piece * PIECE, PIECE), PIECE)],
            dst_ref=crecv.at[n], send_sem=csend.at[n], recv_sem=crsem.at[n],
            device_id=sibling, device_id_type=MESH,
        )
        copy.start()
        core_copies.append(copy)
    xy_copies = []
    for n, piece in enumerate(order):
        core_copies[n].wait_recv()
        total = acc[pl.ds(pl.multiple_of(core * HALF + piece * PIECE, PIECE), PIECE)] + crecv[n]
        if n == len(XY):
            own[...] = total
            break
        p2[n] = total.astype(bf16)
        x, y = xy_peers[n]
        copy = pltpu.make_async_remote_copy(
            src_ref=p2.at[n], dst_ref=xyrecv.at[n], send_sem=xysend.at[n], recv_sem=xyrsem.at[n],
            device_id=device(cz, x, y, core), device_id_type=MESH,
        )
        copy.start()
        xy_copies.append(copy)
    pending += core_copies + xy_copies

    def convolve(out, field, i, weights, order, bias):
        window = jnp.concatenate(
            [
                jnp.concatenate([field[i + p, k + q] for p in order for q in order], axis=0)
                for k in range(NYL)
            ],
            axis=1,
        )
        y = jnp.dot(weights[...], window, preferred_element_type=f32)
        for k in range(NYL):
            low, mid, high = (y[r * C : (r + 1) * C, k * NZ : (k + 1) * NZ] for r in order)
            total = mid + jnp.where(first, 0.0, pltpu.roll(low, 1, axis=1))
            total = total + jnp.where(last, 0.0, pltpu.roll(high, NZ - 1, axis=1))
            out[pl.ds(k, C, stride=NYL), :] = total if bias is None else total + bias

    convolve(vgrad0, cs, 0, wr_ref, (2, 1, 0), None)
    convolve(vgrad1, cs, 1, wr_ref, (2, 1, 0), None)

    for copy in xy_copies:
        copy.wait_recv()
    total = own[...]
    for n in range(len(XY)):
        total = total + xyrecv[n].astype(f32)

    zall[cz] = total.astype(bf16)
    z_copies = []
    for n, z in enumerate(z_peers):
        copy = pltpu.make_async_remote_copy(
            src_ref=zall.at[cz], dst_ref=zall.at[cz], send_sem=zsend.at[n], recv_sem=zrsem.at[n],
            device_id=device(z, cx, cy, core), device_id_type=MESH,
        )
        copy.start()
        z_copies.append(copy)
    pending += z_copies

    square = lax.broadcasted_iota(jnp.int32, (C, C), 0) == lax.broadcasted_iota(jnp.int32, (C, C), 1)
    bias = jnp.sum(jnp.where(square, off_ref[...], 0.0), axis=1, keepdims=True)
    for copy in xs_halo:
        copy.wait_recv()
    convolve(resp0, xs, 0, wf_ref, (0, 1, 2), bias)
    convolve(resp1, xs, 1, wf_ref, (0, 1, 2), bias)

    for copy in z_copies:
        copy.wait_recv()
    total = zall[0].astype(f32)
    for n in range(1, GZ):
        total = total + zall[n].astype(f32)
    gath[core, idx] = (total * factor).astype(bf16)

    def hand_on(n, source):
        return pltpu.make_async_remote_copy(
            src_ref=gath.at[core, source], dst_ref=gath.at[core, source],
            send_sem=fsend.at[n], recv_sem=frsem.at[n], device_id=sibling, device_id_type=MESH,
        )

    gx_copies = []
    for n, (x, y) in enumerate(xy_peers):
        copy = pltpu.make_async_remote_copy(
            src_ref=gath.at[core, idx], dst_ref=gath.at[core, idx],
            send_sem=gxsend.at[n], recv_sem=gxrsem.at[n],
            device_id=device(cz, x, y, core), device_id_type=MESH,
        )
        copy.start()
        gx_copies.append(copy)
    forwards = [hand_on(len(XY), idx)]
    forwards[0].start()
    for n, (dx, dy) in reversed(list(enumerate(XY))):
        gx_copies[n].wait_recv()
        source = lax.rem(cx - dx + GX, GX) * GY + lax.rem(cy - dy + GY, GY)
        forwards.append(hand_on(n, source))
        forwards[-1].start()
    for copy in forwards:
        copy.wait_recv()
    for copy in pending + gx_copies + forwards:
        copy.wait_send()


def finish(resp0, resp1, vgrad0, vgrad1, gath, resp_hbm, vgrad_hbm, filt_hbm, bias_ref, fs, fout, sem):
    copies = []
    for n, (source, out) in enumerate(
        ((resp0, resp_hbm), (resp1, resp_hbm), (vgrad0, vgrad_hbm), (vgrad1, vgrad_hbm))
    ):
        copies.append(pltpu.make_async_copy(source, out.at[:, n % 2], sem.at[n]))
        copies[-1].start()

    def rows(at):
        return gath[pl.ds(at, C), :].astype(jnp.float32)

    bias_ref[...] = gath[pl.ds(BIAS, 16), :].astype(jnp.float32)[:1, :C]
    for r in range(3):
        for p in range(3):
            columns = jnp.concatenate(
                [rows(t * TALL + r * C) for t in (2 * p, 2 * p + 1)]
                + [rows(6 * TALL + r * C)[:, 32 * p : 32 * (p + 1)]],
                axis=1,
            )
            for n, q in enumerate(QS):
                fs[pl.ds(9 * p + 3 * q + r, C, stride=32), :C] = columns[:, n * C : (n + 1) * C]
    for part in range(3):
        for n in range(part * 8, part * 8 + 8):
            parts = [fs[pl.ds((n * 4 + k) * 32, 27), :][:, :C] for k in range(4)]
            fout[:, n * 4 * C : (n + 1) * 4 * C] = jnp.concatenate(parts, axis=1)
        columns = pl.ds(part * 32 * C, 32 * C)
        copies.append(pltpu.make_async_copy(fout.at[:, columns], filt_hbm.at[:, columns], sem.at[4 + part]))
        copies[-1].start()
    for copy in copies:
        copy.wait()


def on_device(volume, filters, offsets, upstream):
    cells = volume.shape[1] * volume.shape[2] * volume.shape[3]
    cells = cells * lax.axis_size("chan") * lax.axis_size("space")
    factor = 1.0 / math.sqrt(cells)
    flat = (C * NXL * NYL, NZ)
    plane = (C * NYL, NZ)
    grid = (NXL + 2, NYL + 2, C, NZ)
    peers, along = GX * GY - 1, GZ - 1
    f32, bf16 = jnp.float32, jnp.bfloat16
    vmem = pl.BlockSpec(memory_space=pltpu.VMEM)
    hbm = pl.BlockSpec(memory_space=pl.ANY)
    dma = pltpu.SemaphoreType.DMA
    resp0, resp1, vgrad0, vgrad1, gath = pl.pallas_call(
        functools.partial(body, factor),
        out_shape=[jax.ShapeDtypeStruct(plane, f32)] * 4
        + [jax.ShapeDtypeStruct((2, GX * GY, PIECE, 128), bf16)],
        in_specs=[hbm, hbm, hbm, vmem],
        out_specs=[vmem] * 5,
        scratch_shapes=[
            pltpu.VMEM(flat, f32),
            pltpu.VMEM(flat, f32),
            pltpu.VMEM((27, C * C), f32),
            pltpu.VMEM((C * 32, 128), f32),
            pltpu.VMEM((TALL, 9 * C), bf16),
            pltpu.VMEM((TALL, 9 * C), bf16),
            pltpu.VMEM(grid, bf16),
            pltpu.VMEM(grid, bf16),
            pltpu.VMEM((NXL, NYL, TALL + 16, NZ), bf16),
            pltpu.VMEM((ROWS, 128), f32),
            pltpu.VMEM((peers + 1, PIECE, 128), f32),
            pltpu.VMEM((peers, PIECE, 128), bf16),
            pltpu.VMEM((peers, PIECE, 128), bf16),
            pltpu.VMEM((PIECE, 128), f32),
            pltpu.VMEM((GZ, PIECE, 128), bf16),
            dma((3,)),
            dma((2, 10)),
            dma((2, 10)),
            dma((peers + 1,)),
            dma((peers + 1,)),
            dma((peers,)),
            dma((peers,)),
            dma((along,)),
            dma((along,)),
            dma((peers,)),
            dma((peers,)),
            dma((peers + 1,)),
            dma((peers + 1,)),
        ],
        compiler_params=pltpu.CompilerParams(
            collective_id=0, has_side_effects=True, vmem_limit_bytes=50 * 1024 * 1024
        ),
    )(volume.reshape(flat), upstream.reshape(flat), filters, offsets.reshape(1, C))
    finished = pl.pallas_call(
        finish,
        out_shape=[
            jax.ShapeDtypeStruct((C, NXL, NYL, NZ), f32),
            jax.ShapeDtypeStruct((C, NXL, NYL, NZ), f32),
            jax.ShapeDtypeStruct((27, C * C), f32),
            jax.ShapeDtypeStruct((1, C), f32),
        ],
        in_specs=[vmem] * 5,
        out_specs=[hbm, hbm, hbm, vmem],
        scratch_shapes=[pltpu.VMEM((C * 32, 128), f32), pltpu.VMEM((27, C * C), f32), dma((7,))],
        compiler_params=pltpu.CompilerParams(vmem_limit_bytes=16 * 1024 * 1024),
    )(*(one.reshape(C, NYL, NZ) for one in (resp0, resp1, vgrad0, vgrad1)), gath.reshape(ROWS, 128))
    resp, vgrad, filter_grad, offset_grad = finished
    return (resp, vgrad, filter_grad, offset_grad.reshape(C))


def solution(mesh):
    placed = (P(None, "chan", "space", None), P(), P(), P(None, "chan", "space", None))
    return jax.shard_map(
        on_device,
        mesh=mesh,
        in_specs=placed,
        out_specs=(P(None, "chan", "space", None), P(None, "chan", "space", None), P(), P()),
        check_vma=False,
    )
```

```python
import functools
import math

import jax
import jax.numpy as jnp
from jax import lax
from jax.experimental import pallas as pl
from jax.experimental.pallas import tpu as pltpu
from jax.sharding import PartitionSpec as P

MESH = pl.DeviceIdType.MESH
C = 96
NXL = 2
NYL = 16
NZ = 128
GX, GY, GZ = 4, 4, 8
TALL = 3 * C
ROWS = 2048
HALF = ROWS // 2
PIECE = HALF // (GX * GY)
BIAS = 7 * TALL
TAPS = 40
HALVES = ((1, 9), (10, 7))
XY = [(dx, dy) for dx in (2, 1, 3, 0) for dy in (2, 1, 3, 0) if (dx, dy) != (0, 0)]
NT = (((1,), (1,)), ((), ()))


def body(factor, vol_hbm, up_hbm, filt_hbm, resp0, resp1, vgrad0, vgrad1, gath,
         vbuf, ubuf, fbuf, fs, wf_ref, wr_ref, xs, cs, x3, acc, crecv, p2, xyrecv, own, zall,
         load_sem, hsend, hrecv, csend, crsem, xysend, xyrsem, zsend, zrsem,
         gxsend, gxrsem, fsend, frsem):
    f32, bf16 = jnp.float32, jnp.bfloat16
    chan = lax.axis_index("chan")
    space = lax.axis_index("space")
    nchan = 4 * GX * GY
    nspace = GZ // 2
    core = lax.rem(chan, 2)
    cy = lax.rem(chan // 2, GY)
    cx = lax.rem(chan // (2 * GY), GX)
    zl = chan // (2 * GY * GX)
    cz = space * 2 + zl
    idx = cx * GY + cy

    def device(z, x, y, k):
        return {"chan": ((lax.rem(z, 2) * GX + x) * GY + y) * 2 + k, "space": z // 2}

    def beside(dc, ds):
        return {"chan": lax.rem(chan + dc + nchan, nchan), "space": lax.rem(space + ds + nspace, nspace)}

    sibling = device(cz, cx, cy, 1 - core)
    xy_peers = [(lax.rem(cx + dx, GX), lax.rem(cy + dy, GY)) for dx, dy in XY]
    z_peers = [lax.rem(cz + dz, GZ) for dz in (4, 3, 5, 2, 6, 1, 7)]

    barrier = pltpu.get_barrier_semaphore()
    everyone = [beside(dc, ds) for dc in (-1, 1, 0) for ds in (-1, 1, 0) if (dc, ds) != (0, 0)]
    everyone += [sibling]
    everyone += [device(cz, x, y, core) for x, y in xy_peers]
    everyone += [device(z, cx, cy, core) for z in z_peers]
    load_up = pltpu.make_async_copy(up_hbm, ubuf, load_sem.at[0])
    load_up.start()
    for one in everyone:
        pl.semaphore_signal(barrier, inc=1, device_id=one, device_id_type=MESH)
    load_vol = pltpu.make_async_copy(vol_hbm, vbuf, load_sem.at[1])
    load_vol.start()
    load_filt = pltpu.make_async_copy(filt_hbm, fbuf, load_sem.at[2])
    load_filt.start()

    lane = lax.broadcasted_iota(jnp.int32, (C, NZ), 1)
    first, last = lane == 0, lane == NZ - 1

    load_up.wait()

    @pl.loop(0, NXL * NYL, unroll=4)
    def _(n):
        v = ubuf[pl.ds(n, C, stride=NXL * NYL), :]
        cs[n // NYL + 1, lax.rem(n, NYL) + 1] = v.astype(bf16)

    pl.semaphore_wait(barrier, len(everyone))
    pending = []

    def inside(dc, ds):
        ok = None
        for d, at, count in ((dc, chan, nchan), (ds, space, nspace)):
            if d != 0:
                here = at < count - 1 if d > 0 else at > 0
                ok = here if ok is None else jnp.logical_and(ok, here)
        return ok

    class Halo:
        def __init__(self, field, which, n, dc, ds, row, count):
            plane_from, plane_to, planes = {-1: (1, NXL + 1, 1), 0: (1, 1, NXL), 1: (NXL, 0, 1)}[dc]
            row_from, row_to = {-1: (1, NYL + 1), 0: (row, row), 1: (NYL, 0)}[ds]
            self.copy = pltpu.make_async_remote_copy(
                src_ref=field.at[pl.ds(plane_from, planes), pl.ds(row_from, count)],
                dst_ref=field.at[pl.ds(plane_to, planes), pl.ds(row_to, count)],
                send_sem=hsend.at[which, n], recv_sem=hrecv.at[which, n],
                device_id=beside(dc, ds), device_id_type=MESH,
            )
            self.to, self.source = inside(dc, ds), inside(-dc, -ds)

        def start(self):
            pl.when(self.to)(self.copy.start)

        def wait_recv(self):
            pl.when(self.source)(self.copy.wait_recv)

        def wait_send(self):
            pl.when(self.to)(self.copy.wait_send)

    def halo(field, which):
        sides = [(0, ds, 0, 1) for ds in (-1, 1)]
        sides += [(dc, ds, 0, 1) for dc in (-1, 1) for ds in (-1, 1)]
        sides += [(dc, 0, row, count) for row, count in HALVES for dc in (-1, 1)]
        return [Halo(field, which, n, *side) for n, side in enumerate(sides)]

    cs_halo = halo(cs, 0)
    for copy in cs_halo:
        copy.start()
    pending += cs_halo

    for field in (cs, xs):
        @pl.when(chan == 0)
        def _():
            field[0] = jnp.zeros((NYL + 2, C, NZ), bf16)

        @pl.when(chan == nchan - 1)
        def _():
            field[NXL + 1] = jnp.zeros((NYL + 2, C, NZ), bf16)

        @pl.when(space == 0)
        def _():
            for n in range(NXL + 2):
                field[n, 0] = jnp.zeros((C, NZ), bf16)

        @pl.when(space == nspace - 1)
        def _():
            for n in range(NXL + 2):
                field[n, NYL + 1] = jnp.zeros((C, NZ), bf16)

    load_vol.wait()

    @pl.loop(0, NXL * NYL, unroll=4)
    def _(n):
        i, j = n // NYL, lax.rem(n, NYL)
        v = vbuf[pl.ds(n, C, stride=NXL * NYL), :]
        rounded = v.astype(bf16)
        xs[i + 1, j + 1] = rounded
        x3[i, j, pl.ds(C, C)] = rounded
        x3[i, j, pl.ds(0, C)] = jnp.where(first, 0.0, pltpu.roll(v, 1, axis=1)).astype(bf16)
        x3[i, j, pl.ds(2 * C, C)] = jnp.where(last, 0.0, pltpu.roll(v, NZ - 1, axis=1)).astype(bf16)
        x3[i, j, pl.ds(TALL, 16)] = jnp.ones((16, NZ), bf16)

    acc[pl.ds(6 * TALL, TALL)] = jnp.zeros((TALL, 128), f32)
    acc[pl.ds(BIAS, 32)] = jnp.zeros((32, 128), f32)
    step = NYL // 2

    def shifted(i, j):
        return jnp.concatenate([x3[i, j + k] for k in range(step)], axis=1)

    def terms(i, j, p, fresh):
        def rows(k):
            low, mid, high = (cs[i + 2 - p, j + k + 2 - q] for q in range(3))
            return jnp.concatenate([mid, high[:32], low, high[32:64]], axis=0)

        right = jnp.concatenate([rows(k) for k in range(step)], axis=1)
        v = lax.dot_general(shifted(i, j), right, NT, preferred_element_type=f32)
        for t in range(2):
            at = pl.ds((2 * p + t) * TALL, TALL)
            part = v[:TALL, t * 128 : (t + 1) * 128]
            acc[at] = part if fresh else acc[at] + part
        if p == 1:
            acc[pl.ds(BIAS, 16)] += v[TALL:, :128]

    def rest(i, j):
        def rows(k):
            return jnp.concatenate([cs[i + 2 - p, j + k][C - 32 :] for p in range(3)], axis=0)

        right = jnp.concatenate([rows(k) for k in range(step)], axis=1)
        v = lax.dot_general(shifted(i, j), right, NT, preferred_element_type=f32)
        acc[pl.ds(6 * TALL, TALL), : 3 * 32] += v[:TALL]

    rows_halo, corner_halo, plane_halo = cs_halo[:2], cs_halo[2:6], cs_halo[6:]
    for copy in rows_halo:
        copy.wait_recv()
    for j in (0, step):
        terms(0, j, 0, j == 0)
        terms(0, j, 1, j == 0)
        terms(1, j, 1, False)
        terms(1, j, 2, j == 0)

    load_filt.wait()

    for n in range(C // 4):
        v = fbuf[:, n * 4 * C : (n + 1) * 4 * C]
        for k in range(4):
            fs[pl.ds((n * 4 + k) * 32, 27), :C] = v[:, k * C : (k + 1) * C]
    for r in range(3):
        taps = [fs[pl.ds(3 * n + r, C, stride=32), :][:, :C] for n in range(9)]
        wr_ref[pl.ds(r * C, C), :] = jnp.concatenate(taps, axis=1).astype(bf16)
        wf_ref[pl.ds(r * C, C), :] = jnp.concatenate([tap.T for tap in taps], axis=1).astype(bf16)

    for copy in corner_halo + plane_halo[:2]:
        copy.wait_recv()
    xs_halo = halo(xs, 1)
    for part in range(2):
        if part == 1:
            for copy in plane_halo[2:]:
                copy.wait_recv()
        j = part * step
        terms(0, j, 2, False)
        terms(1, j, 0, False)
        rest(0, j)
        rest(1, j)

    order = [x * GY + y for x, y in xy_peers] + [idx]
    core_copies = []
    for n, piece in enumerate(order):
        copy = pltpu.make_async_remote_copy(
            src_ref=acc.at[pl.ds(pl.multiple_of((1 - core) * HALF + piece * PIECE, PIECE), PIECE)],
            dst_ref=crecv.at[n], send_sem=csend.at[n], recv_sem=crsem.at[n],
            device_id=sibling, device_id_type=MESH,
        )
        copy.start()
        core_copies.append(copy)
    xy_copies = []
    for n, piece in enumerate(order):
        core_copies[n].wait_recv()
        total = acc[pl.ds(pl.multiple_of(core * HALF + piece * PIECE, PIECE), PIECE)] + crecv[n]
        if n == len(XY):
            own[...] = total
            break
        p2[n] = total.astype(bf16)
        x, y = xy_peers[n]
        copy = pltpu.make_async_remote_copy(
            src_ref=p2.at[n], dst_ref=xyrecv.at[n], send_sem=xysend.at[n], recv_sem=xyrsem.at[n],
            device_id=device(cz, x, y, core), device_id_type=MESH,
        )
        copy.start()
        xy_copies.append(copy)
    pending += core_copies + xy_copies + xs_halo
    for copy in xs_halo[:8]:
        copy.start()

    def convolve(out, field, i, weights, order):
        window = jnp.concatenate(
            [
                jnp.concatenate([field[i + p, k + q] for p in order for q in order], axis=0)
                for k in range(NYL)
            ],
            axis=1,
        )
        y = jnp.dot(weights[...], window, preferred_element_type=f32)
        for k in range(NYL):
            low, mid, high = (y[r * C : (r + 1) * C, k * NZ : (k + 1) * NZ] for r in order)
            total = mid + jnp.where(first, 0.0, pltpu.roll(low, 1, axis=1))
            total = total + jnp.where(last, 0.0, pltpu.roll(high, NZ - 1, axis=1))
            out[pl.ds(k, C, stride=NYL), :] = total

    convolve(vgrad0, cs, 0, wr_ref, (2, 1, 0))
    convolve(vgrad1, cs, 1, wr_ref, (2, 1, 0))

    for copy in xy_copies:
        copy.wait_recv()
    total = own[...]
    for n in range(len(XY)):
        total = total + xyrecv[n].astype(f32)

    zall[cz] = total.astype(bf16)
    z_copies = []
    for n, z in enumerate(z_peers):
        copy = pltpu.make_async_remote_copy(
            src_ref=zall.at[cz], dst_ref=zall.at[cz], send_sem=zsend.at[n], recv_sem=zrsem.at[n],
            device_id=device(z, cx, cy, core), device_id_type=MESH,
        )
        copy.start()
        z_copies.append(copy)
    pending += z_copies
    for copy in xs_halo[8:]:
        copy.start()

    for copy in z_copies:
        copy.wait_recv()
    total = zall[0].astype(f32)
    for n in range(1, GZ):
        total = total + zall[n].astype(f32)
    gath[core, idx] = (total * factor).astype(bf16)

    def hand_on(n, source):
        return pltpu.make_async_remote_copy(
            src_ref=gath.at[core, source], dst_ref=gath.at[core, source],
            send_sem=fsend.at[n], recv_sem=frsem.at[n], device_id=sibling, device_id_type=MESH,
        )

    gx_copies = []
    for n, (x, y) in enumerate(xy_peers):
        copy = pltpu.make_async_remote_copy(
            src_ref=gath.at[core, idx], dst_ref=gath.at[core, idx],
            send_sem=gxsend.at[n], recv_sem=gxrsem.at[n],
            device_id=device(cz, x, y, core), device_id_type=MESH,
        )
        copy.start()
        gx_copies.append(copy)
    forwards = [hand_on(len(XY), idx)]
    forwards[0].start()
    for copy in xs_halo:
        copy.wait_recv()
    convolve(resp0, xs, 0, wf_ref, (0, 1, 2))
    convolve(resp1, xs, 1, wf_ref, (0, 1, 2))
    for n, (dx, dy) in reversed(list(enumerate(XY))):
        gx_copies[n].wait_recv()
        source = lax.rem(cx - dx + GX, GX) * GY + lax.rem(cy - dy + GY, GY)
        forwards.append(hand_on(n, source))
        forwards[-1].start()
    for copy in forwards:
        copy.wait_recv()
    for copy in pending + gx_copies + forwards:
        copy.wait_send()


def finish(off_ref, resp0, resp1, vgrad0, vgrad1, gath, resp_hbm, vgrad_hbm, filt_hbm, bias_ref,
           out0, out1, column, fs, fout, sem):
    copies = []

    def send(source, out):
        copies.append(pltpu.make_async_copy(source, out, sem.at[len(copies)]))
        copies[-1].start()

    send(vgrad0, vgrad_hbm.at[:, 0])
    send(vgrad1, vgrad_hbm.at[:, 1])
    square = lax.broadcasted_iota(jnp.int32, (C, C), 0) == lax.broadcasted_iota(jnp.int32, (C, C), 1)
    offset = jnp.sum(jnp.where(square, off_ref[...], 0.0), axis=1, keepdims=True)
    column[...] = jnp.broadcast_to(offset, (C, NZ))
    for n, (source, out) in enumerate(((resp0, out0), (resp1, out1))):
        for c in range(C):
            out[c] = source[c] + column[pl.ds(c, 1), :]
        send(out, resp_hbm.at[:, n])

    def rows(at):
        return gath[pl.ds(at, C), :].astype(jnp.float32)

    bias_ref[...] = gath[pl.ds(BIAS, 16), :].astype(jnp.float32)[:1, :C]
    for r in range(3):
        last = rows(6 * TALL + r * C)
        for p in range(3):
            mid, low = rows(2 * p * TALL + r * C), rows((2 * p + 1) * TALL + r * C)
            high = jnp.concatenate([mid[:, C:], low[:, C:], last[:, 32 * p : 32 * (p + 1)]], axis=1)
            for q, part in enumerate((low[:, :C], mid[:, :C], high)):
                fs[pl.ds(9 * p + 3 * q + r, C, stride=TAPS), :C] = part
    for part in range(3):
        for n in range(part * 8, part * 8 + 8):
            parts = [fs[pl.ds((n * 4 + k) * TAPS, 27), :][:, :C] for k in range(4)]
            fout[:, n * 4 * C : (n + 1) * 4 * C] = jnp.concatenate(parts, axis=1)
        columns = pl.ds(part * 32 * C, 32 * C)
        send(fout.at[:, columns], filt_hbm.at[:, columns])
    for copy in copies:
        copy.wait()


def on_device(volume, filters, offsets, upstream):
    cells = volume.shape[1] * volume.shape[2] * volume.shape[3]
    cells = cells * lax.axis_size("chan") * lax.axis_size("space")
    factor = 1.0 / math.sqrt(cells)
    flat = (C * NXL * NYL, NZ)
    plane = (C * NYL, NZ)
    grid = (NXL + 2, NYL + 2, C, NZ)
    peers, along = GX * GY - 1, GZ - 1
    f32, bf16 = jnp.float32, jnp.bfloat16
    vmem = pl.BlockSpec(memory_space=pltpu.VMEM)
    hbm = pl.BlockSpec(memory_space=pl.ANY)
    dma = pltpu.SemaphoreType.DMA
    resp0, resp1, vgrad0, vgrad1, gath = pl.pallas_call(
        functools.partial(body, factor),
        out_shape=[jax.ShapeDtypeStruct(plane, f32)] * 4
        + [jax.ShapeDtypeStruct((2, GX * GY, PIECE, 128), bf16)],
        in_specs=[hbm, hbm, hbm],
        out_specs=[vmem] * 5,
        scratch_shapes=[
            pltpu.VMEM(flat, f32),
            pltpu.VMEM(flat, f32),
            pltpu.VMEM((27, C * C), f32),
            pltpu.VMEM((C * 32, 128), f32),
            pltpu.VMEM((TALL, 9 * C), bf16),
            pltpu.VMEM((TALL, 9 * C), bf16),
            pltpu.VMEM(grid, bf16),
            pltpu.VMEM(grid, bf16),
            pltpu.VMEM((NXL, NYL, TALL + 16, NZ), bf16),
            pltpu.VMEM((ROWS, 128), f32),
            pltpu.VMEM((peers + 1, PIECE, 128), f32),
            pltpu.VMEM((peers, PIECE, 128), bf16),
            pltpu.VMEM((peers, PIECE, 128), bf16),
            pltpu.VMEM((PIECE, 128), f32),
            pltpu.VMEM((GZ, PIECE, 128), bf16),
            dma((3,)),
            dma((2, 10)),
            dma((2, 10)),
            dma((peers + 1,)),
            dma((peers + 1,)),
            dma((peers,)),
            dma((peers,)),
            dma((along,)),
            dma((along,)),
            dma((peers,)),
            dma((peers,)),
            dma((peers + 1,)),
            dma((peers + 1,)),
        ],
        compiler_params=pltpu.CompilerParams(
            collective_id=0, has_side_effects=True, vmem_limit_bytes=50 * 1024 * 1024
        ),
    )(volume.reshape(flat), upstream.reshape(flat), filters)
    finished = pl.pallas_call(
        finish,
        out_shape=[
            jax.ShapeDtypeStruct((C, NXL, NYL, NZ), f32),
            jax.ShapeDtypeStruct((C, NXL, NYL, NZ), f32),
            jax.ShapeDtypeStruct((27, C * C), f32),
            jax.ShapeDtypeStruct((1, C), f32),
        ],
        in_specs=[vmem] * 6,
        out_specs=[hbm, hbm, hbm, vmem],
        scratch_shapes=[
            pltpu.VMEM((C, NYL, NZ), f32),
            pltpu.VMEM((C, NYL, NZ), f32),
            pltpu.VMEM((C, NZ), f32),
            pltpu.VMEM((C * TAPS, 128), f32),
            pltpu.VMEM((27, C * C), f32),
            dma((7,)),
        ],
        compiler_params=pltpu.CompilerParams(vmem_limit_bytes=16 * 1024 * 1024),
    )(offsets.reshape(1, C), *(one.reshape(C, NYL, NZ) for one in (resp0, resp1, vgrad0, vgrad1)), gath.reshape(ROWS, 128))
    resp, vgrad, filter_grad, offset_grad = finished
    return (resp, vgrad, filter_grad, offset_grad.reshape(C))


def solution(mesh):
    placed = (P(None, "chan", "space", None), P(), P(), P(None, "chan", "space", None))
    return jax.shard_map(
        on_device,
        mesh=mesh,
        in_specs=placed,
        out_specs=(P(None, "chan", "space", None), P(None, "chan", "space", None), P(), P()),
        check_vma=False,
    )
```

```python
import functools
import math

import jax
import jax.numpy as jnp
from jax import lax
from jax.experimental import pallas as pl
from jax.experimental.pallas import tpu as pltpu
from jax.sharding import PartitionSpec as P

MESH = pl.DeviceIdType.MESH
C = 96
NXL = 2
NYL = 16
NZ = 128
GX, GY, GZ = 4, 4, 8
TALL = 3 * C
ROWS = 2048
HALF = ROWS // 2
PIECE = HALF // (GX * GY)
BIAS = 7 * TALL
TAPS = 40
HALVES = ((1, 9), (10, 7))
FAR = (2, 1, 3, 0)
XY = [(dx, dy) for dx in FAR for dy in FAR if (dx, dy) != (0, 0)]
NT = (((1,), (1,)), ((), ()))


def body(factor, vol_hbm, up_hbm, filt_hbm, resp0, resp1, vgrad0, vgrad1, gath,
         vbuf, ubuf, fbuf, fs, wf_ref, wr_ref, xs, cs, x3, acc, crecv, p2, xyrecv, own, zall,
         load_sem, hsend, hrecv, csend, crsem, xysend, xyrsem, zsend, zrsem,
         gxsend, gxrsem, fsend, frsem):
    f32, bf16 = jnp.float32, jnp.bfloat16
    chan = lax.axis_index("chan")
    space = lax.axis_index("space")
    nchan = 4 * GX * GY
    nspace = GZ // 2
    core = lax.rem(chan, 2)
    cy = lax.rem(chan // 2, GY)
    cx = lax.rem(chan // (2 * GY), GX)
    zl = chan // (2 * GY * GX)
    cz = space * 2 + zl
    idx = cx * GY + cy

    def device(z, x, y, k):
        return {"chan": ((lax.rem(z, 2) * GX + x) * GY + y) * 2 + k, "space": z // 2}

    def beside(dc, ds):
        return {"chan": lax.rem(chan + dc + nchan, nchan), "space": lax.rem(space + ds + nspace, nspace)}

    sibling = device(cz, cx, cy, 1 - core)
    xy_peers = [(lax.rem(cx + dx, GX), lax.rem(cy + dy, GY)) for dx, dy in XY]
    z_peers = [lax.rem(cz + dz, GZ) for dz in (4, 3, 5, 2, 6, 1, 7)]

    barrier = pltpu.get_barrier_semaphore()
    everyone = [beside(dc, ds) for dc in (-1, 1, 0) for ds in (-1, 1, 0) if (dc, ds) != (0, 0)]
    everyone += [sibling]
    everyone += [device(cz, x, y, core) for x, y in xy_peers]
    everyone += [device(z, cx, cy, core) for z in z_peers]
    load_up = pltpu.make_async_copy(up_hbm, ubuf, load_sem.at[0])
    load_up.start()
    for one in everyone:
        pl.semaphore_signal(barrier, inc=1, device_id=one, device_id_type=MESH)
    load_vol = pltpu.make_async_copy(vol_hbm, vbuf, load_sem.at[1])
    load_vol.start()
    load_filt = pltpu.make_async_copy(filt_hbm, fbuf, load_sem.at[2])
    load_filt.start()

    lane = lax.broadcasted_iota(jnp.int32, (C, NZ), 1)
    first, last = lane == 0, lane == NZ - 1

    load_up.wait()

    @pl.loop(0, NXL * NYL, unroll=4)
    def _(n):
        v = ubuf[pl.ds(n, C, stride=NXL * NYL), :]
        cs[n // NYL + 1, lax.rem(n, NYL) + 1] = v.astype(bf16)

    pl.semaphore_wait(barrier, len(everyone))
    pending = []

    def inside(dc, ds):
        ok = None
        for d, at, count in ((dc, chan, nchan), (ds, space, nspace)):
            if d != 0:
                here = at < count - 1 if d > 0 else at > 0
                ok = here if ok is None else jnp.logical_and(ok, here)
        return ok

    class Halo:
        def __init__(self, field, which, n, dc, ds, row, count):
            plane_from, plane_to, planes = {-1: (1, NXL + 1, 1), 0: (1, 1, NXL), 1: (NXL, 0, 1)}[dc]
            row_from, row_to = {-1: (1, NYL + 1), 0: (row, row), 1: (NYL, 0)}[ds]
            self.copy = pltpu.make_async_remote_copy(
                src_ref=field.at[pl.ds(plane_from, planes), pl.ds(row_from, count)],
                dst_ref=field.at[pl.ds(plane_to, planes), pl.ds(row_to, count)],
                send_sem=hsend.at[which, n], recv_sem=hrecv.at[which, n],
                device_id=beside(dc, ds), device_id_type=MESH,
            )
            self.to, self.source = inside(dc, ds), inside(-dc, -ds)

        def start(self):
            pl.when(self.to)(self.copy.start)

        def wait_recv(self):
            pl.when(self.source)(self.copy.wait_recv)

        def wait_send(self):
            pl.when(self.to)(self.copy.wait_send)

    def halo(field, which):
        sides = [(0, ds, 0, 1) for ds in (-1, 1)]
        sides += [(dc, ds, 0, 1) for dc in (-1, 1) for ds in (-1, 1)]
        sides += [(dc, 0, row, count) for row, count in HALVES for dc in (-1, 1)]
        return [Halo(field, which, n, *side) for n, side in enumerate(sides)]

    cs_halo = halo(cs, 0)
    for copy in cs_halo:
        copy.start()
    pending += cs_halo

    for field in (cs, xs):
        @pl.when(chan == 0)
        def _():
            field[0] = jnp.zeros((NYL + 2, C, NZ), bf16)

        @pl.when(chan == nchan - 1)
        def _():
            field[NXL + 1] = jnp.zeros((NYL + 2, C, NZ), bf16)

        @pl.when(space == 0)
        def _():
            for n in range(NXL + 2):
                field[n, 0] = jnp.zeros((C, NZ), bf16)

        @pl.when(space == nspace - 1)
        def _():
            for n in range(NXL + 2):
                field[n, NYL + 1] = jnp.zeros((C, NZ), bf16)

    load_vol.wait()

    @pl.loop(0, NXL * NYL, unroll=4)
    def _(n):
        i, j = n // NYL, lax.rem(n, NYL)
        v = vbuf[pl.ds(n, C, stride=NXL * NYL), :]
        rounded = v.astype(bf16)
        xs[i + 1, j + 1] = rounded
        x3[i, j, pl.ds(C, C)] = rounded
        x3[i, j, pl.ds(0, C)] = jnp.where(first, 0.0, pltpu.roll(v, 1, axis=1)).astype(bf16)
        x3[i, j, pl.ds(2 * C, C)] = jnp.where(last, 0.0, pltpu.roll(v, NZ - 1, axis=1)).astype(bf16)
        x3[i, j, pl.ds(TALL, 16)] = jnp.ones((16, NZ), bf16)

    acc[pl.ds(6 * TALL, TALL)] = jnp.zeros((TALL, 128), f32)
    acc[pl.ds(BIAS, 32)] = jnp.zeros((32, 128), f32)
    step = NYL // 2

    def shifted(i, j):
        return jnp.concatenate([x3[i, j + k] for k in range(step)], axis=1)

    def terms(i, j, p, fresh):
        def rows(k):
            low, mid, high = (cs[i + 2 - p, j + k + 2 - q] for q in range(3))
            return jnp.concatenate([mid, high[:32], low, high[32:64]], axis=0)

        right = jnp.concatenate([rows(k) for k in range(step)], axis=1)
        v = lax.dot_general(shifted(i, j), right, NT, preferred_element_type=f32)
        for t in range(2):
            at = pl.ds((2 * p + t) * TALL, TALL)
            part = v[:TALL, t * 128 : (t + 1) * 128]
            acc[at] = part if fresh else acc[at] + part
        if p == 1:
            acc[pl.ds(BIAS, 16)] += v[TALL:, :128]

    def rest(i, j):
        def rows(k):
            return jnp.concatenate([cs[i + 2 - p, j + k][C - 32 :] for p in range(3)], axis=0)

        right = jnp.concatenate([rows(k) for k in range(step)], axis=1)
        v = lax.dot_general(shifted(i, j), right, NT, preferred_element_type=f32)
        acc[pl.ds(6 * TALL, TALL), : 3 * 32] += v[:TALL]

    rows_halo, corner_halo, plane_halo = cs_halo[:2], cs_halo[2:6], cs_halo[6:]
    for copy in rows_halo:
        copy.wait_recv()
    for j in (0, step):
        terms(0, j, 0, j == 0)
        terms(0, j, 1, j == 0)
        terms(1, j, 1, False)
        terms(1, j, 2, j == 0)

    load_filt.wait()

    for n in range(C // 4):
        v = fbuf[:, n * 4 * C : (n + 1) * 4 * C]
        for k in range(4):
            fs[pl.ds((n * 4 + k) * 32, 27), :C] = v[:, k * C : (k + 1) * C]
    for r in range(3):
        taps = [fs[pl.ds(3 * n + r, C, stride=32), :][:, :C] for n in range(9)]
        wr_ref[pl.ds(r * C, C), :] = jnp.concatenate(taps, axis=1).astype(bf16)
        wf_ref[pl.ds(r * C, C), :] = jnp.concatenate([tap.T for tap in taps], axis=1).astype(bf16)

    for copy in corner_halo + plane_halo[:2]:
        copy.wait_recv()
    xs_halo = halo(xs, 1)
    for part in range(2):
        if part == 1:
            for copy in plane_halo[2:]:
                copy.wait_recv()
        j = part * step
        terms(0, j, 2, False)
        terms(1, j, 0, False)
        rest(0, j)
        rest(1, j)

    core_copies = []
    for n, dx in enumerate(FAR):
        at = pl.multiple_of(lax.rem(cx + dx, GX) * GY * PIECE, GY * PIECE)
        copy = pltpu.make_async_remote_copy(
            src_ref=acc.at[pl.ds((1 - core) * HALF + at, GY * PIECE)],
            dst_ref=crecv.at[n], send_sem=csend.at[n], recv_sem=crsem.at[n],
            device_id=sibling, device_id_type=MESH,
        )
        copy.start()
        core_copies.append(copy)
    xy_copies = []
    for n, dx in enumerate(FAR):
        core_copies[n].wait_recv()
        x = lax.rem(cx + dx, GX)
        for dy in FAR:
            y = lax.rem(cy + dy, GY)
            at = pl.multiple_of(core * HALF + (x * GY + y) * PIECE, PIECE)
            total = acc[pl.ds(at, PIECE)] + crecv[n, pl.ds(pl.multiple_of(y * PIECE, PIECE), PIECE)]
            if (dx, dy) == (0, 0):
                own[...] = total
                continue
            m = XY.index((dx, dy))
            p2[m] = total.astype(bf16)
            copy = pltpu.make_async_remote_copy(
                src_ref=p2.at[m], dst_ref=xyrecv.at[m], send_sem=xysend.at[m], recv_sem=xyrsem.at[m],
                device_id=device(cz, x, y, core), device_id_type=MESH,
            )
            copy.start()
            xy_copies.append(copy)
    pending += core_copies
    for copy in xs_halo[:8]:
        copy.start()

    def convolve(out, field, i, weights, order):
        window = jnp.concatenate(
            [
                jnp.concatenate([field[i + p, k + q] for p in order for q in order], axis=0)
                for k in range(NYL)
            ],
            axis=1,
        )
        y = jnp.dot(weights[...], window, preferred_element_type=f32)
        for k in range(NYL):
            low, mid, high = (y[r * C : (r + 1) * C, k * NZ : (k + 1) * NZ] for r in order)
            total = mid + jnp.where(first, 0.0, pltpu.roll(low, 1, axis=1))
            total = total + jnp.where(last, 0.0, pltpu.roll(high, NZ - 1, axis=1))
            out[pl.ds(k, C, stride=NYL), :] = total

    convolve(vgrad0, cs, 0, wr_ref, (2, 1, 0))
    convolve(vgrad1, cs, 1, wr_ref, (2, 1, 0))

    for copy in pending:
        copy.wait_send()
    for copy in xy_copies:
        copy.wait_recv()
    total = own[...]
    for n in range(len(XY)):
        total = total + xyrecv[n].astype(f32)

    zall[cz] = total.astype(bf16)
    z_copies = []
    for n, z in enumerate(z_peers):
        copy = pltpu.make_async_remote_copy(
            src_ref=zall.at[cz], dst_ref=zall.at[cz], send_sem=zsend.at[n], recv_sem=zrsem.at[n],
            device_id=device(z, cx, cy, core), device_id_type=MESH,
        )
        copy.start()
        z_copies.append(copy)
    for copy in xs_halo[8:]:
        copy.start()

    for copy in xy_copies:
        copy.wait_send()
    for copy in z_copies:
        copy.wait_recv()
    total = zall[0].astype(f32)
    for n in range(1, GZ):
        total = total + zall[n].astype(f32)
    gath[core, idx] = (total * factor).astype(bf16)

    gx_copies = []
    for n, (x, y) in enumerate(xy_peers):
        copy = pltpu.make_async_remote_copy(
            src_ref=gath.at[core, idx], dst_ref=gath.at[core, idx],
            send_sem=gxsend.at[n], recv_sem=gxrsem.at[n],
            device_id=device(cz, x, y, core), device_id_type=MESH,
        )
        copy.start()
        gx_copies.append(copy)
    for copy in z_copies + xs_halo:
        copy.wait_send()
    for copy in xs_halo:
        copy.wait_recv()
    convolve(resp0, xs, 0, wf_ref, (0, 1, 2))
    convolve(resp1, xs, 1, wf_ref, (0, 1, 2))
    forwards = []
    for dx in (0, 1, 3, 2):
        for n in range(len(XY)):
            if XY[n][0] == dx:
                gx_copies[n].wait_recv()
        source = pl.ds(lax.rem(cx - dx + GX, GX) * GY, GY)
        copy = pltpu.make_async_remote_copy(
            src_ref=gath.at[core, source], dst_ref=gath.at[core, source],
            send_sem=fsend.at[dx], recv_sem=frsem.at[dx], device_id=sibling, device_id_type=MESH,
        )
        copy.start()
        forwards.append(copy)
    for copy in forwards:
        copy.wait_recv()
    for copy in gx_copies + forwards:
        copy.wait_send()


def finish(off_ref, resp0, resp1, vgrad0, vgrad1, gath, resp_hbm, vgrad_hbm, filt_hbm, bias_ref,
           out0, out1, column, fs, fout, sem):
    copies = []

    def send(source, out):
        copies.append(pltpu.make_async_copy(source, out, sem.at[len(copies)]))
        copies[-1].start()

    send(vgrad0, vgrad_hbm.at[:, 0])
    send(vgrad1, vgrad_hbm.at[:, 1])
    square = lax.broadcasted_iota(jnp.int32, (C, C), 0) == lax.broadcasted_iota(jnp.int32, (C, C), 1)
    offset = jnp.sum(jnp.where(square, off_ref[...], 0.0), axis=1, keepdims=True)
    column[...] = jnp.broadcast_to(offset, (C, NZ))
    for n, (source, out) in enumerate(((resp0, out0), (resp1, out1))):
        for c in range(C):
            out[c] = source[c] + column[pl.ds(c, 1), :]
        send(out, resp_hbm.at[:, n])

    def rows(at):
        return gath[pl.ds(at, C), :].astype(jnp.float32)

    bias_ref[...] = gath[pl.ds(BIAS, 16), :].astype(jnp.float32)[:1, :C]
    for r in range(3):
        last = rows(6 * TALL + r * C)
        for p in range(3):
            mid, low = rows(2 * p * TALL + r * C), rows((2 * p + 1) * TALL + r * C)
            high = jnp.concatenate([mid[:, C:], low[:, C:], last[:, 32 * p : 32 * (p + 1)]], axis=1)
            for q, part in enumerate((low[:, :C], mid[:, :C], high)):
                fs[pl.ds(9 * p + 3 * q + r, C, stride=TAPS), :C] = part
    for part in range(3):
        for n in range(part * 8, part * 8 + 8):
            parts = [fs[pl.ds((n * 4 + k) * TAPS, 27), :][:, :C] for k in range(4)]
            fout[:, n * 4 * C : (n + 1) * 4 * C] = jnp.concatenate(parts, axis=1)
        columns = pl.ds(part * 32 * C, 32 * C)
        send(fout.at[:, columns], filt_hbm.at[:, columns])
    for copy in copies:
        copy.wait()


def on_device(volume, filters, offsets, upstream):
    cells = volume.shape[1] * volume.shape[2] * volume.shape[3]
    cells = cells * lax.axis_size("chan") * lax.axis_size("space")
    factor = 1.0 / math.sqrt(cells)
    flat = (C * NXL * NYL, NZ)
    plane = (C * NYL, NZ)
    grid = (NXL + 2, NYL + 2, C, NZ)
    peers, along = GX * GY - 1, GZ - 1
    f32, bf16 = jnp.float32, jnp.bfloat16
    vmem = pl.BlockSpec(memory_space=pltpu.VMEM)
    hbm = pl.BlockSpec(memory_space=pl.ANY)
    dma = pltpu.SemaphoreType.DMA
    resp0, resp1, vgrad0, vgrad1, gath = pl.pallas_call(
        functools.partial(body, factor),
        out_shape=[jax.ShapeDtypeStruct(plane, f32)] * 4
        + [jax.ShapeDtypeStruct((2, GX * GY, PIECE, 128), bf16)],
        in_specs=[hbm, hbm, hbm],
        out_specs=[vmem] * 5,
        scratch_shapes=[
            pltpu.VMEM(flat, f32),
            pltpu.VMEM(flat, f32),
            pltpu.VMEM((27, C * C), f32),
            pltpu.VMEM((C * 32, 128), f32),
            pltpu.VMEM((TALL, 9 * C), bf16),
            pltpu.VMEM((TALL, 9 * C), bf16),
            pltpu.VMEM(grid, bf16),
            pltpu.VMEM(grid, bf16),
            pltpu.VMEM((NXL, NYL, TALL + 16, NZ), bf16),
            pltpu.VMEM((ROWS, 128), f32),
            pltpu.VMEM((GX, GY * PIECE, 128), f32),
            pltpu.VMEM((peers, PIECE, 128), bf16),
            pltpu.VMEM((peers, PIECE, 128), bf16),
            pltpu.VMEM((PIECE, 128), f32),
            pltpu.VMEM((GZ, PIECE, 128), bf16),
            dma((3,)),
            dma((2, 10)),
            dma((2, 10)),
            dma((GX,)),
            dma((GX,)),
            dma((peers,)),
            dma((peers,)),
            dma((along,)),
            dma((along,)),
            dma((peers,)),
            dma((peers,)),
            dma((GX,)),
            dma((GX,)),
        ],
        compiler_params=pltpu.CompilerParams(
            collective_id=0, has_side_effects=True, vmem_limit_bytes=50 * 1024 * 1024
        ),
    )(volume.reshape(flat), upstream.reshape(flat), filters)
    finished = pl.pallas_call(
        finish,
        out_shape=[
            jax.ShapeDtypeStruct((C, NXL, NYL, NZ), f32),
            jax.ShapeDtypeStruct((C, NXL, NYL, NZ), f32),
            jax.ShapeDtypeStruct((27, C * C), f32),
            jax.ShapeDtypeStruct((1, C), f32),
        ],
        in_specs=[vmem] * 6,
        out_specs=[hbm, hbm, hbm, vmem],
        scratch_shapes=[
            pltpu.VMEM((C, NYL, NZ), f32),
            pltpu.VMEM((C, NYL, NZ), f32),
            pltpu.VMEM((C, NZ), f32),
            pltpu.VMEM((C * TAPS, 128), f32),
            pltpu.VMEM((27, C * C), f32),
            dma((7,)),
        ],
        compiler_params=pltpu.CompilerParams(vmem_limit_bytes=16 * 1024 * 1024),
    )(offsets.reshape(1, C), *(one.reshape(C, NYL, NZ) for one in (resp0, resp1, vgrad0, vgrad1)), gath.reshape(ROWS, 128))
    resp, vgrad, filter_grad, offset_grad = finished
    return (resp, vgrad, filter_grad, offset_grad.reshape(C))


def solution(mesh):
    placed = (P(None, "chan", "space", None), P(), P(), P(None, "chan", "space", None))
    return jax.shard_map(
        on_device,
        mesh=mesh,
        in_specs=placed,
        out_specs=(P(None, "chan", "space", None), P(None, "chan", "space", None), P(), P()),
        check_vma=False,
    )
```

```python
import functools
import math

import jax
import jax.numpy as jnp
from jax import lax
from jax.experimental import pallas as pl
from jax.experimental.pallas import tpu as pltpu
from jax.sharding import PartitionSpec as P

MESH = pl.DeviceIdType.MESH
C = 96
NXL = 2
NYL = 16
NZ = 128
GX, GY, GZ = 4, 4, 8
TALL = 3 * C
ROWS = 2048
HALF = ROWS // 2
PIECE = HALF // (GX * GY)
BIAS = 7 * TALL
TAPS = 40
HALVES = ((1, 9), (10, 7))
FAR = (2, 1, 3, 0)
XY = [(dx, dy) for dx in FAR for dy in FAR if (dx, dy) != (0, 0)]
NT = (((1,), (1,)), ((), ()))


def body(factor, vol_hbm, up_hbm, filt_hbm, resp0, resp1, vgrad0, vgrad1, gath,
         vbuf, ubuf, fbuf, fs, wf_ref, wr_ref, xs, cs, x3, acc, crecv, p2, xyrecv, own, zall,
         load_sem, hsend, hrecv, csend, crsem, xysend, xyrsem, zsend, zrsem,
         gxsend, gxrsem, fsend, frsem):
    f32, bf16 = jnp.float32, jnp.bfloat16
    chan = lax.axis_index("chan")
    space = lax.axis_index("space")
    nchan = 4 * GX * GY
    nspace = GZ // 2
    core = lax.rem(chan, 2)
    cy = lax.rem(chan // 2, GY)
    cx = lax.rem(chan // (2 * GY), GX)
    zl = chan // (2 * GY * GX)
    cz = space * 2 + zl
    idx = cx * GY + cy

    def device(z, x, y, k):
        return {"chan": ((lax.rem(z, 2) * GX + x) * GY + y) * 2 + k, "space": z // 2}

    def beside(dc, ds):
        return {"chan": lax.rem(chan + dc + nchan, nchan), "space": lax.rem(space + ds + nspace, nspace)}

    sibling = device(cz, cx, cy, 1 - core)
    xy_peers = [(lax.rem(cx + dx, GX), lax.rem(cy + dy, GY)) for dx, dy in XY]
    z_peers = [lax.rem(cz + dz, GZ) for dz in (4, 3, 5, 2, 6, 1, 7)]

    barrier = pltpu.get_barrier_semaphore()
    everyone = [beside(dc, ds) for dc in (-1, 1, 0) for ds in (-1, 1, 0) if (dc, ds) != (0, 0)]
    everyone += [sibling]
    everyone += [device(cz, x, y, core) for x, y in xy_peers]
    everyone += [device(z, cx, cy, core) for z in z_peers]
    load_up = pltpu.make_async_copy(up_hbm, ubuf, load_sem.at[0])
    load_up.start()
    for one in everyone:
        pl.semaphore_signal(barrier, inc=1, device_id=one, device_id_type=MESH)
    load_vol = pltpu.make_async_copy(vol_hbm, vbuf, load_sem.at[1])
    load_vol.start()
    load_filt = pltpu.make_async_copy(filt_hbm, fbuf, load_sem.at[2])
    load_filt.start()

    lane = lax.broadcasted_iota(jnp.int32, (C, NZ), 1)
    first, last = lane == 0, lane == NZ - 1

    load_up.wait()

    @pl.loop(0, NXL * NYL, unroll=4)
    def _(n):
        v = ubuf[pl.ds(n, C, stride=NXL * NYL), :]
        cs[n // NYL + 1, lax.rem(n, NYL) + 1] = v.astype(bf16)

    pl.semaphore_wait(barrier, len(everyone))
    pending = []

    def inside(dc, ds):
        ok = None
        for d, at, count in ((dc, chan, nchan), (ds, space, nspace)):
            if d != 0:
                here = at < count - 1 if d > 0 else at > 0
                ok = here if ok is None else jnp.logical_and(ok, here)
        return ok

    class Halo:
        def __init__(self, field, which, n, dc, ds, row, count):
            plane_from, plane_to, planes = {-1: (1, NXL + 1, 1), 0: (1, 1, NXL), 1: (NXL, 0, 1)}[dc]
            row_from, row_to = {-1: (1, NYL + 1), 0: (row, row), 1: (NYL, 0)}[ds]
            self.copy = pltpu.make_async_remote_copy(
                src_ref=field.at[pl.ds(plane_from, planes), pl.ds(row_from, count)],
                dst_ref=field.at[pl.ds(plane_to, planes), pl.ds(row_to, count)],
                send_sem=hsend.at[which, n], recv_sem=hrecv.at[which, n],
                device_id=beside(dc, ds), device_id_type=MESH,
            )
            self.to, self.source = inside(dc, ds), inside(-dc, -ds)

        def start(self):
            pl.when(self.to)(self.copy.start)

        def wait_recv(self):
            pl.when(self.source)(self.copy.wait_recv)

        def wait_send(self):
            pl.when(self.to)(self.copy.wait_send)

    def halo(field, which):
        sides = [(0, ds, 0, 1) for ds in (-1, 1)]
        sides += [(dc, ds, 0, 1) for dc in (-1, 1) for ds in (-1, 1)]
        sides += [(dc, 0, row, count) for row, count in HALVES for dc in (-1, 1)]
        return [Halo(field, which, n, *side) for n, side in enumerate(sides)]

    cs_halo = halo(cs, 0)
    for copy in cs_halo:
        copy.start()
    pending += cs_halo

    for field in (cs, xs):
        @pl.when(chan == 0)
        def _():
            field[0] = jnp.zeros((NYL + 2, C, NZ), bf16)

        @pl.when(chan == nchan - 1)
        def _():
            field[NXL + 1] = jnp.zeros((NYL + 2, C, NZ), bf16)

        @pl.when(space == 0)
        def _():
            for n in range(NXL + 2):
                field[n, 0] = jnp.zeros((C, NZ), bf16)

        @pl.when(space == nspace - 1)
        def _():
            for n in range(NXL + 2):
                field[n, NYL + 1] = jnp.zeros((C, NZ), bf16)

    load_vol.wait()

    @pl.loop(0, NXL * NYL, unroll=4)
    def _(n):
        i, j = n // NYL, lax.rem(n, NYL)
        v = vbuf[pl.ds(n, C, stride=NXL * NYL), :]
        rounded = v.astype(bf16)
        xs[i + 1, j + 1] = rounded
        x3[i, j, pl.ds(C, C)] = rounded
        x3[i, j, pl.ds(0, C)] = jnp.where(first, 0.0, pltpu.roll(v, 1, axis=1)).astype(bf16)
        x3[i, j, pl.ds(2 * C, C)] = jnp.where(last, 0.0, pltpu.roll(v, NZ - 1, axis=1)).astype(bf16)
        x3[i, j, pl.ds(TALL, 16)] = jnp.ones((16, NZ), bf16)

    acc[pl.ds(6 * TALL, TALL)] = jnp.zeros((TALL, 128), f32)
    acc[pl.ds(BIAS, 32)] = jnp.zeros((32, 128), f32)
    step = NYL // 2

    def shifted(i, j):
        return jnp.concatenate([x3[i, j + k] for k in range(step)], axis=1)

    def terms(i, j, p, fresh):
        def rows(k):
            low, mid, high = (cs[i + 2 - p, j + k + 2 - q] for q in range(3))
            return jnp.concatenate([mid, high[:32], low, high[32:64]], axis=0)

        right = jnp.concatenate([rows(k) for k in range(step)], axis=1)
        v = lax.dot_general(shifted(i, j), right, NT, preferred_element_type=f32)
        for t in range(2):
            at = pl.ds((2 * p + t) * TALL, TALL)
            part = v[:TALL, t * 128 : (t + 1) * 128]
            acc[at] = part if fresh else acc[at] + part
        if p == 1:
            acc[pl.ds(BIAS, 16)] += v[TALL:, :128]

    def rest(i, j):
        def rows(k):
            return jnp.concatenate([cs[i + 2 - p, j + k][C - 32 :] for p in range(3)], axis=0)

        right = jnp.concatenate([rows(k) for k in range(step)], axis=1)
        v = lax.dot_general(shifted(i, j), right, NT, preferred_element_type=f32)
        acc[pl.ds(6 * TALL, TALL), : 3 * 32] += v[:TALL]

    rows_halo, corner_halo, plane_halo = cs_halo[:2], cs_halo[2:6], cs_halo[6:]
    for copy in rows_halo:
        copy.wait_recv()
    for j in (0, step):
        terms(0, j, 0, j == 0)
        terms(0, j, 1, j == 0)
        terms(1, j, 1, False)
        terms(1, j, 2, j == 0)

    load_filt.wait()

    for n in range(C // 4):
        v = fbuf[:, n * 4 * C : (n + 1) * 4 * C]
        for k in range(4):
            fs[pl.ds((n * 4 + k) * 32, 27), :C] = v[:, k * C : (k + 1) * C]
    for r in range(3):
        taps = [fs[pl.ds(3 * n + r, C, stride=32), :][:, :C] for n in range(9)]
        wr_ref[pl.ds(r * C, C), :] = jnp.concatenate(taps, axis=1).astype(bf16)
        wf_ref[pl.ds(r * C, C), :] = jnp.concatenate([tap.T for tap in taps], axis=1).astype(bf16)

    for copy in corner_halo + plane_halo[:2]:
        copy.wait_recv()
    xs_halo = halo(xs, 1)
    for part in range(2):
        if part == 1:
            for copy in plane_halo[2:]:
                copy.wait_recv()
        j = part * step
        terms(0, j, 2, False)
        terms(1, j, 0, False)
        rest(0, j)
        rest(1, j)

    core_copies = []
    for n, dx in enumerate(FAR):
        at = pl.multiple_of(lax.rem(cx + dx, GX) * GY * PIECE, GY * PIECE)
        copy = pltpu.make_async_remote_copy(
            src_ref=acc.at[pl.ds((1 - core) * HALF + at, GY * PIECE)],
            dst_ref=crecv.at[n], send_sem=csend.at[n], recv_sem=crsem.at[n],
            device_id=sibling, device_id_type=MESH,
        )
        copy.start()
        core_copies.append(copy)
    xy_copies = []
    for n, dx in enumerate(FAR):
        core_copies[n].wait_recv()
        x = lax.rem(cx + dx, GX)
        for dy in FAR:
            y = lax.rem(cy + dy, GY)
            at = pl.multiple_of(core * HALF + (x * GY + y) * PIECE, PIECE)
            total = acc[pl.ds(at, PIECE)] + crecv[n, pl.ds(pl.multiple_of(y * PIECE, PIECE), PIECE)]
            if (dx, dy) == (0, 0):
                own[...] = total
                continue
            m = XY.index((dx, dy))
            p2[m] = total.astype(bf16)
            copy = pltpu.make_async_remote_copy(
                src_ref=p2.at[m], dst_ref=xyrecv.at[m], send_sem=xysend.at[m], recv_sem=xyrsem.at[m],
                device_id=device(cz, x, y, core), device_id_type=MESH,
            )
            copy.start()
            xy_copies.append(copy)
    pending += core_copies
    for copy in xs_halo[:8]:
        copy.start()

    def convolve(out, field, i, weights, order, start=0, count=NYL):
        window = jnp.concatenate(
            [
                jnp.concatenate([field[i + p, start + k + q] for p in order for q in order], axis=0)
                for k in range(count)
            ],
            axis=1,
        )
        y = jnp.dot(weights[...], window, preferred_element_type=f32)
        for k in range(count):
            low, mid, high = (y[r * C : (r + 1) * C, k * NZ : (k + 1) * NZ] for r in order)
            total = mid + jnp.where(first, 0.0, pltpu.roll(low, 1, axis=1))
            total = total + jnp.where(last, 0.0, pltpu.roll(high, NZ - 1, axis=1))
            out[pl.ds(start + k, C, stride=NYL), :] = total

    convolve(vgrad0, cs, 0, wr_ref, (2, 1, 0))
    convolve(vgrad1, cs, 1, wr_ref, (2, 1, 0))

    for copy in pending:
        copy.wait_send()
    for copy in xy_copies:
        copy.wait_recv()
    total = own[...]
    for n in range(len(XY)):
        total = total + xyrecv[n].astype(f32)

    zall[cz] = total.astype(bf16)
    z_copies = []
    for n, z in enumerate(z_peers):
        copy = pltpu.make_async_remote_copy(
            src_ref=zall.at[cz], dst_ref=zall.at[cz], send_sem=zsend.at[n], recv_sem=zrsem.at[n],
            device_id=device(z, cx, cy, core), device_id_type=MESH,
        )
        copy.start()
        z_copies.append(copy)
    for copy in xs_halo[8:]:
        copy.start()

    for copy in xy_copies + xs_halo[:8]:
        copy.wait_send()
    for copy in xs_halo[:8]:
        copy.wait_recv()
    half = NYL // 2
    convolve(resp0, xs, 0, wf_ref, (0, 1, 2), 0, half)
    convolve(resp1, xs, 1, wf_ref, (0, 1, 2), 0, half)
    for copy in z_copies:
        copy.wait_recv()
    total = zall[0].astype(f32)
    for n in range(1, GZ):
        total = total + zall[n].astype(f32)
    gath[core, idx] = (total * factor).astype(bf16)

    gx_copies = []
    for n, (x, y) in enumerate(xy_peers):
        copy = pltpu.make_async_remote_copy(
            src_ref=gath.at[core, idx], dst_ref=gath.at[core, idx],
            send_sem=gxsend.at[n], recv_sem=gxrsem.at[n],
            device_id=device(cz, x, y, core), device_id_type=MESH,
        )
        copy.start()
        gx_copies.append(copy)
    for copy in z_copies + xs_halo[8:]:
        copy.wait_send()
    for copy in xs_halo[8:]:
        copy.wait_recv()
    convolve(resp0, xs, 0, wf_ref, (0, 1, 2), half, half)
    convolve(resp1, xs, 1, wf_ref, (0, 1, 2), half, half)
    forwards = []
    for dx in (0, 1, 3, 2):
        for n in range(len(XY)):
            if XY[n][0] == dx:
                gx_copies[n].wait_recv()
        source = pl.ds(lax.rem(cx - dx + GX, GX) * GY, GY)
        copy = pltpu.make_async_remote_copy(
            src_ref=gath.at[core, source], dst_ref=gath.at[core, source],
            send_sem=fsend.at[dx], recv_sem=frsem.at[dx], device_id=sibling, device_id_type=MESH,
        )
        copy.start()
        forwards.append(copy)
    for copy in forwards:
        copy.wait_recv()
    for copy in gx_copies + forwards:
        copy.wait_send()


def finish(off_ref, resp0, resp1, vgrad0, vgrad1, gath, resp_hbm, vgrad_hbm, filt_hbm, bias_ref,
           out0, out1, column, fs, fout, sem):
    copies = []

    def send(source, out):
        copies.append(pltpu.make_async_copy(source, out, sem.at[len(copies)]))
        copies[-1].start()

    send(vgrad0, vgrad_hbm.at[:, 0])
    send(vgrad1, vgrad_hbm.at[:, 1])
    square = lax.broadcasted_iota(jnp.int32, (C, C), 0) == lax.broadcasted_iota(jnp.int32, (C, C), 1)
    offset = jnp.sum(jnp.where(square, off_ref[...], 0.0), axis=1, keepdims=True)
    column[...] = jnp.broadcast_to(offset, (C, NZ))
    for n, (source, out) in enumerate(((resp0, out0), (resp1, out1))):
        for c in range(C):
            out[c] = source[c] + column[pl.ds(c, 1), :]
        send(out, resp_hbm.at[:, n])

    def rows(at):
        return gath[pl.ds(at, C), :].astype(jnp.float32)

    bias_ref[...] = gath[pl.ds(BIAS, 16), :].astype(jnp.float32)[:1, :C]
    for r in range(3):
        last = rows(6 * TALL + r * C)
        for p in range(3):
            mid, low = rows(2 * p * TALL + r * C), rows((2 * p + 1) * TALL + r * C)
            high = jnp.concatenate([mid[:, C:], low[:, C:], last[:, 32 * p : 32 * (p + 1)]], axis=1)
            for q, part in enumerate((low[:, :C], mid[:, :C], high)):
                fs[pl.ds(9 * p + 3 * q + r, C, stride=TAPS), :C] = part
    for part in range(3):
        for n in range(part * 8, part * 8 + 8):
            parts = [fs[pl.ds((n * 4 + k) * TAPS, 27), :][:, :C] for k in range(4)]
            fout[:, n * 4 * C : (n + 1) * 4 * C] = jnp.concatenate(parts, axis=1)
        columns = pl.ds(part * 32 * C, 32 * C)
        send(fout.at[:, columns], filt_hbm.at[:, columns])
    for copy in copies:
        copy.wait()


def on_device(volume, filters, offsets, upstream):
    cells = volume.shape[1] * volume.shape[2] * volume.shape[3]
    cells = cells * lax.axis_size("chan") * lax.axis_size("space")
    factor = 1.0 / math.sqrt(cells)
    flat = (C * NXL * NYL, NZ)
    plane = (C * NYL, NZ)
    grid = (NXL + 2, NYL + 2, C, NZ)
    peers, along = GX * GY - 1, GZ - 1
    f32, bf16 = jnp.float32, jnp.bfloat16
    vmem = pl.BlockSpec(memory_space=pltpu.VMEM)
    hbm = pl.BlockSpec(memory_space=pl.ANY)
    dma = pltpu.SemaphoreType.DMA
    resp0, resp1, vgrad0, vgrad1, gath = pl.pallas_call(
        functools.partial(body, factor),
        out_shape=[jax.ShapeDtypeStruct(plane, f32)] * 4
        + [jax.ShapeDtypeStruct((2, GX * GY, PIECE, 128), bf16)],
        in_specs=[hbm, hbm, hbm],
        out_specs=[vmem] * 5,
        scratch_shapes=[
            pltpu.VMEM(flat, f32),
            pltpu.VMEM(flat, f32),
            pltpu.VMEM((27, C * C), f32),
            pltpu.VMEM((C * 32, 128), f32),
            pltpu.VMEM((TALL, 9 * C), bf16),
            pltpu.VMEM((TALL, 9 * C), bf16),
            pltpu.VMEM(grid, bf16),
            pltpu.VMEM(grid, bf16),
            pltpu.VMEM((NXL, NYL, TALL + 16, NZ), bf16),
            pltpu.VMEM((ROWS, 128), f32),
            pltpu.VMEM((GX, GY * PIECE, 128), f32),
            pltpu.VMEM((peers, PIECE, 128), bf16),
            pltpu.VMEM((peers, PIECE, 128), bf16),
            pltpu.VMEM((PIECE, 128), f32),
            pltpu.VMEM((GZ, PIECE, 128), bf16),
            dma((3,)),
            dma((2, 10)),
            dma((2, 10)),
            dma((GX,)),
            dma((GX,)),
            dma((peers,)),
            dma((peers,)),
            dma((along,)),
            dma((along,)),
            dma((peers,)),
            dma((peers,)),
            dma((GX,)),
            dma((GX,)),
        ],
        compiler_params=pltpu.CompilerParams(
            collective_id=0, has_side_effects=True, vmem_limit_bytes=50 * 1024 * 1024
        ),
    )(volume.reshape(flat), upstream.reshape(flat), filters)
    finished = pl.pallas_call(
        finish,
        out_shape=[
            jax.ShapeDtypeStruct((C, NXL, NYL, NZ), f32),
            jax.ShapeDtypeStruct((C, NXL, NYL, NZ), f32),
            jax.ShapeDtypeStruct((27, C * C), f32),
            jax.ShapeDtypeStruct((1, C), f32),
        ],
        in_specs=[vmem] * 6,
        out_specs=[hbm, hbm, hbm, vmem],
        scratch_shapes=[
            pltpu.VMEM((C, NYL, NZ), f32),
            pltpu.VMEM((C, NYL, NZ), f32),
            pltpu.VMEM((C, NZ), f32),
            pltpu.VMEM((C * TAPS, 128), f32),
            pltpu.VMEM((27, C * C), f32),
            dma((7,)),
        ],
        compiler_params=pltpu.CompilerParams(vmem_limit_bytes=16 * 1024 * 1024),
    )(offsets.reshape(1, C), *(one.reshape(C, NYL, NZ) for one in (resp0, resp1, vgrad0, vgrad1)), gath.reshape(ROWS, 128))
    resp, vgrad, filter_grad, offset_grad = finished
    return (resp, vgrad, filter_grad, offset_grad.reshape(C))


def solution(mesh):
    placed = (P(None, "chan", "space", None), P(), P(), P(None, "chan", "space", None))
    return jax.shard_map(
        on_device,
        mesh=mesh,
        in_specs=placed,
        out_specs=(P(None, "chan", "space", None), P(None, "chan", "space", None), P(), P()),
        check_vma=False,
    )
```

```python
import functools
import math

import jax
import jax.numpy as jnp
from jax import lax
from jax.experimental import pallas as pl
from jax.experimental.pallas import tpu as pltpu
from jax.sharding import PartitionSpec as P

MESH = pl.DeviceIdType.MESH
C = 96
NXL = 2
NYL = 16
NZ = 128
GX, GY, GZ = 4, 4, 8
TALL = 3 * C
ROWS = 2048
HALF = ROWS // 2
PIECE = HALF // (GX * GY)
BIAS = 7 * TALL
TAPS = 40
HALVES = ((1, 9), (10, 7))
FAR = (2, 1, 3, 0)
XY = [(dx, dy) for dx in FAR for dy in FAR if (dx, dy) != (0, 0)]
NT = (((1,), (1,)), ((), ()))


def body(factor, vol_hbm, up_hbm, filt_hbm, resp0, resp1, vgrad0, vgrad1, gath,
         vbuf, ubuf, fbuf, fs, wf_ref, wr_ref, xs, cs, x3, acc, give, crecv, p2, xyrecv, own, zall,
         load_sem, hsend, hrecv, csend, crsem, xysend, xyrsem, zsend, zrsem,
         gxsend, gxrsem, fsend, frsem):
    f32, bf16 = jnp.float32, jnp.bfloat16
    chan = lax.axis_index("chan")
    space = lax.axis_index("space")
    nchan = 4 * GX * GY
    nspace = GZ // 2
    core = lax.rem(chan, 2)
    cy = lax.rem(chan // 2, GY)
    cx = lax.rem(chan // (2 * GY), GX)
    zl = chan // (2 * GY * GX)
    cz = space * 2 + zl
    idx = cx * GY + cy

    def device(z, x, y, k):
        return {"chan": ((lax.rem(z, 2) * GX + x) * GY + y) * 2 + k, "space": z // 2}

    def beside(dc, ds):
        return {"chan": lax.rem(chan + dc + nchan, nchan), "space": lax.rem(space + ds + nspace, nspace)}

    sibling = device(cz, cx, cy, 1 - core)
    xy_peers = [(lax.rem(cx + dx, GX), lax.rem(cy + dy, GY)) for dx, dy in XY]
    z_peers = [lax.rem(cz + dz, GZ) for dz in (4, 3, 5, 2, 6, 1, 7)]

    barrier = pltpu.get_barrier_semaphore()
    everyone = [beside(dc, ds) for dc in (-1, 1, 0) for ds in (-1, 1, 0) if (dc, ds) != (0, 0)]
    everyone += [device(cz, x, y, core) for x, y in xy_peers]
    everyone += [device(z, cx, cy, core) for z in [lax.rem(cz + dz, GZ) for dz in (4, 3, 5, 1, 7)]]
    load_up = pltpu.make_async_copy(up_hbm, ubuf, load_sem.at[0])
    load_up.start()
    for one in everyone:
        pl.semaphore_signal(barrier, inc=1, device_id=one, device_id_type=MESH)
    load_vol = pltpu.make_async_copy(vol_hbm, vbuf, load_sem.at[1])
    load_vol.start()
    load_filt = pltpu.make_async_copy(filt_hbm, fbuf, load_sem.at[2])
    load_filt.start()

    lane = lax.broadcasted_iota(jnp.int32, (C, NZ), 1)
    first, last = lane == 0, lane == NZ - 1

    load_up.wait()

    @pl.loop(0, NXL * NYL, unroll=4)
    def _(n):
        v = ubuf[pl.ds(n, C, stride=NXL * NYL), :]
        cs[n // NYL + 1, lax.rem(n, NYL) + 1] = v.astype(bf16)

    pl.semaphore_wait(barrier, len(everyone))
    pending = []

    def inside(dc, ds):
        ok = None
        for d, at, count in ((dc, chan, nchan), (ds, space, nspace)):
            if d != 0:
                here = at < count - 1 if d > 0 else at > 0
                ok = here if ok is None else jnp.logical_and(ok, here)
        return ok

    class Halo:
        def __init__(self, field, which, n, dc, ds, row, count):
            plane_from, plane_to, planes = {-1: (1, NXL + 1, 1), 0: (1, 1, NXL), 1: (NXL, 0, 1)}[dc]
            row_from, row_to = {-1: (1, NYL + 1), 0: (row, row), 1: (NYL, 0)}[ds]
            self.copy = pltpu.make_async_remote_copy(
                src_ref=field.at[pl.ds(plane_from, planes), pl.ds(row_from, count)],
                dst_ref=field.at[pl.ds(plane_to, planes), pl.ds(row_to, count)],
                send_sem=hsend.at[which, n], recv_sem=hrecv.at[which, n],
                device_id=beside(dc, ds), device_id_type=MESH,
            )
            self.to, self.source = inside(dc, ds), inside(-dc, -ds)

        def start(self):
            pl.when(self.to)(self.copy.start)

        def wait_recv(self):
            pl.when(self.source)(self.copy.wait_recv)

        def wait_send(self):
            pl.when(self.to)(self.copy.wait_send)

    def halo(field, which):
        sides = [(0, ds, 0, 1) for ds in (-1, 1)]
        sides += [(dc, ds, 0, 1) for dc in (-1, 1) for ds in (-1, 1)]
        sides += [(dc, 0, row, count) for row, count in HALVES for dc in (-1, 1)]
        return [Halo(field, which, n, *side) for n, side in enumerate(sides)]

    cs_halo = halo(cs, 0)
    for copy in cs_halo:
        copy.start()
    pending += cs_halo

    for field in (cs, xs):
        @pl.when(chan == 0)
        def _():
            field[0] = jnp.zeros((NYL + 2, C, NZ), bf16)

        @pl.when(chan == nchan - 1)
        def _():
            field[NXL + 1] = jnp.zeros((NYL + 2, C, NZ), bf16)

        @pl.when(space == 0)
        def _():
            for n in range(NXL + 2):
                field[n, 0] = jnp.zeros((C, NZ), bf16)

        @pl.when(space == nspace - 1)
        def _():
            for n in range(NXL + 2):
                field[n, NYL + 1] = jnp.zeros((C, NZ), bf16)

    load_vol.wait()

    @pl.loop(0, NXL * NYL, unroll=4)
    def _(n):
        i, j = n // NYL, lax.rem(n, NYL)
        v = vbuf[pl.ds(n, C, stride=NXL * NYL), :]
        rounded = v.astype(bf16)
        xs[i + 1, j + 1] = rounded
        x3[i, j, pl.ds(C, C)] = rounded
        x3[i, j, pl.ds(0, C)] = jnp.where(first, 0.0, pltpu.roll(v, 1, axis=1)).astype(bf16)
        x3[i, j, pl.ds(2 * C, C)] = jnp.where(last, 0.0, pltpu.roll(v, NZ - 1, axis=1)).astype(bf16)
        x3[i, j, pl.ds(TALL, 16)] = jnp.ones((16, NZ), bf16)

    acc[pl.ds(6 * TALL, TALL)] = jnp.zeros((TALL, 128), f32)
    acc[pl.ds(BIAS, 32)] = jnp.zeros((32, 128), f32)
    step = NYL // 2

    def shifted(i, j):
        return jnp.concatenate([x3[i, j + k] for k in range(step)], axis=1)

    def terms(i, j, p, fresh):
        def rows(k):
            low, mid, high = (cs[i + 2 - p, j + k + 2 - q] for q in range(3))
            return jnp.concatenate([mid, high[:32], low, high[32:64]], axis=0)

        right = jnp.concatenate([rows(k) for k in range(step)], axis=1)
        v = lax.dot_general(shifted(i, j), right, NT, preferred_element_type=f32)
        for t in range(2):
            at = pl.ds((2 * p + t) * TALL, TALL)
            part = v[:TALL, t * 128 : (t + 1) * 128]
            acc[at] = part if fresh else acc[at] + part
        if p == 1:
            acc[pl.ds(BIAS, 16)] += v[TALL:, :128]

    def rest(i, j):
        def rows(k):
            return jnp.concatenate([cs[i + 2 - p, j + k][C - 32 :] for p in range(3)], axis=0)

        right = jnp.concatenate([rows(k) for k in range(step)], axis=1)
        v = lax.dot_general(shifted(i, j), right, NT, preferred_element_type=f32)
        acc[pl.ds(6 * TALL, TALL), : 3 * 32] += v[:TALL]

    rows_halo, corner_halo, plane_halo = cs_halo[:2], cs_halo[2:6], cs_halo[6:]
    for copy in rows_halo:
        copy.wait_recv()
    for j in (0, step):
        terms(0, j, 0, j == 0)
        terms(0, j, 1, j == 0)
        terms(1, j, 1, False)
        terms(1, j, 2, j == 0)

    load_filt.wait()

    for n in range(C // 4):
        v = fbuf[:, n * 4 * C : (n + 1) * 4 * C]
        for k in range(4):
            fs[pl.ds((n * 4 + k) * 32, 27), :C] = v[:, k * C : (k + 1) * C]
    for r in range(3):
        taps = [fs[pl.ds(3 * n + r, C, stride=32), :][:, :C] for n in range(9)]
        wr_ref[pl.ds(r * C, C), :] = jnp.concatenate(taps, axis=1).astype(bf16)
        wf_ref[pl.ds(r * C, C), :] = jnp.concatenate([tap.T for tap in taps], axis=1).astype(bf16)

    for copy in corner_halo + plane_halo[:2]:
        copy.wait_recv()
    xs_halo = halo(xs, 1)
    for part in range(2):
        if part == 1:
            for copy in plane_halo[2:]:
                copy.wait_recv()
        j = part * step
        terms(0, j, 2, False)
        terms(1, j, 0, False)
        rest(0, j)
        rest(1, j)

    core_copies = []
    for n, dx in enumerate(FAR):
        at = pl.multiple_of((1 - core) * HALF + lax.rem(cx + dx, GX) * GY * PIECE, GY * PIECE)
        give[n] = acc[pl.ds(at, GY * PIECE)].astype(bf16)
        copy = pltpu.make_async_remote_copy(
            src_ref=give.at[n], dst_ref=crecv.at[n], send_sem=csend.at[n], recv_sem=crsem.at[n],
            device_id=sibling, device_id_type=MESH,
        )
        copy.start()
        core_copies.append(copy)
    xy_copies = []
    for n, dx in enumerate(FAR):
        core_copies[n].wait_recv()
        x = lax.rem(cx + dx, GX)
        for dy in FAR:
            y = lax.rem(cy + dy, GY)
            at = pl.multiple_of(core * HALF + (x * GY + y) * PIECE, PIECE)
            take = crecv[n, pl.ds(pl.multiple_of(y * PIECE, PIECE), PIECE)].astype(f32)
            total = acc[pl.ds(at, PIECE)] + take
            if (dx, dy) == (0, 0):
                own[...] = total
                continue
            m = XY.index((dx, dy))
            p2[m] = total.astype(bf16)
            copy = pltpu.make_async_remote_copy(
                src_ref=p2.at[m], dst_ref=xyrecv.at[m], send_sem=xysend.at[m], recv_sem=xyrsem.at[m],
                device_id=device(cz, x, y, core), device_id_type=MESH,
            )
            copy.start()
            xy_copies.append(copy)
    pending += core_copies
    for copy in xs_halo[:8]:
        copy.start()

    def convolve(out, field, i, weights, order, start=0, count=NYL):
        window = jnp.concatenate(
            [
                jnp.concatenate([field[i + p, start + k + q] for p in order for q in order], axis=0)
                for k in range(count)
            ],
            axis=1,
        )
        y = jnp.dot(weights[...], window, preferred_element_type=f32)
        for k in range(count):
            low, mid, high = (y[r * C : (r + 1) * C, k * NZ : (k + 1) * NZ] for r in order)
            total = mid + jnp.where(first, 0.0, pltpu.roll(low, 1, axis=1))
            total = total + jnp.where(last, 0.0, pltpu.roll(high, NZ - 1, axis=1))
            out[pl.ds(start + k, C, stride=NYL), :] = total

    convolve(vgrad0, cs, 0, wr_ref, (2, 1, 0))
    convolve(vgrad1, cs, 1, wr_ref, (2, 1, 0))

    for copy in pending:
        copy.wait_send()
    for copy in xy_copies:
        copy.wait_recv()
    total = own[...]
    for n in range(len(XY)):
        total = total + xyrecv[n].astype(f32)

    zall[cz] = total.astype(bf16)
    z_copies = []
    for n, z in enumerate(z_peers):
        copy = pltpu.make_async_remote_copy(
            src_ref=zall.at[cz], dst_ref=zall.at[cz], send_sem=zsend.at[n], recv_sem=zrsem.at[n],
            device_id=device(z, cx, cy, core), device_id_type=MESH,
        )
        copy.start()
        z_copies.append(copy)
    for copy in xs_halo[8:]:
        copy.start()

    for copy in xy_copies + xs_halo[:8]:
        copy.wait_send()
    for copy in xs_halo[:8]:
        copy.wait_recv()
    half = NYL // 2
    convolve(resp0, xs, 0, wf_ref, (0, 1, 2), 0, half)
    convolve(resp1, xs, 1, wf_ref, (0, 1, 2), 0, half)
    for copy in z_copies:
        copy.wait_recv()
    total = zall[0].astype(f32)
    for n in range(1, GZ):
        total = total + zall[n].astype(f32)
    gath[core, idx] = (total * factor).astype(bf16)

    gx_copies = []
    for n, (x, y) in enumerate(xy_peers):
        copy = pltpu.make_async_remote_copy(
            src_ref=gath.at[core, idx], dst_ref=gath.at[core, idx],
            send_sem=gxsend.at[n], recv_sem=gxrsem.at[n],
            device_id=device(cz, x, y, core), device_id_type=MESH,
        )
        copy.start()
        gx_copies.append(copy)
    for copy in z_copies + xs_halo[8:]:
        copy.wait_send()
    for copy in xs_halo[8:]:
        copy.wait_recv()
    convolve(resp0, xs, 0, wf_ref, (0, 1, 2), half, half)
    convolve(resp1, xs, 1, wf_ref, (0, 1, 2), half, half)
    forwards = []
    for dx in (0, 1, 3, 2):
        for n in range(len(XY)):
            if XY[n][0] == dx:
                gx_copies[n].wait_recv()
        source = pl.ds(lax.rem(cx - dx + GX, GX) * GY, GY)
        copy = pltpu.make_async_remote_copy(
            src_ref=gath.at[core, source], dst_ref=gath.at[core, source],
            send_sem=fsend.at[dx], recv_sem=frsem.at[dx], device_id=sibling, device_id_type=MESH,
        )
        copy.start()
        forwards.append(copy)
    for copy in forwards:
        copy.wait_recv()
    for copy in gx_copies + forwards:
        copy.wait_send()


def finish(off_ref, resp0, resp1, vgrad0, vgrad1, gath, resp_hbm, vgrad_hbm, filt_hbm, bias_ref,
           out0, out1, column, fs, fout, sem):
    copies = []

    def send(source, out):
        copies.append(pltpu.make_async_copy(source, out, sem.at[len(copies)]))
        copies[-1].start()

    send(vgrad0, vgrad_hbm.at[:, 0])
    send(vgrad1, vgrad_hbm.at[:, 1])
    square = lax.broadcasted_iota(jnp.int32, (C, C), 0) == lax.broadcasted_iota(jnp.int32, (C, C), 1)
    offset = jnp.sum(jnp.where(square, off_ref[...], 0.0), axis=1, keepdims=True)
    column[...] = jnp.broadcast_to(offset, (C, NZ))
    for n, (source, out) in enumerate(((resp0, out0), (resp1, out1))):
        for c in range(C):
            out[c] = source[c] + column[pl.ds(c, 1), :]
        send(out, resp_hbm.at[:, n])

    def rows(at):
        return gath[pl.ds(at, C), :].astype(jnp.float32)

    bias_ref[...] = gath[pl.ds(BIAS, 16), :].astype(jnp.float32)[:1, :C]
    for r in range(3):
        last = rows(6 * TALL + r * C)
        for p in range(3):
            mid, low = rows(2 * p * TALL + r * C), rows((2 * p + 1) * TALL + r * C)
            high = jnp.concatenate([mid[:, C:], low[:, C:], last[:, 32 * p : 32 * (p + 1)]], axis=1)
            for q, part in enumerate((low[:, :C], mid[:, :C], high)):
                fs[pl.ds(9 * p + 3 * q + r, C, stride=TAPS), :C] = part
    for part in range(3):
        for n in range(part * 8, part * 8 + 8):
            parts = [fs[pl.ds((n * 4 + k) * TAPS, 27), :][:, :C] for k in range(4)]
            fout[:, n * 4 * C : (n + 1) * 4 * C] = jnp.concatenate(parts, axis=1)
        columns = pl.ds(part * 32 * C, 32 * C)
        send(fout.at[:, columns], filt_hbm.at[:, columns])
    for copy in copies:
        copy.wait()


def on_device(volume, filters, offsets, upstream):
    cells = volume.shape[1] * volume.shape[2] * volume.shape[3]
    cells = cells * lax.axis_size("chan") * lax.axis_size("space")
    factor = 1.0 / math.sqrt(cells)
    flat = (C * NXL * NYL, NZ)
    plane = (C * NYL, NZ)
    grid = (NXL + 2, NYL + 2, C, NZ)
    peers, along = GX * GY - 1, GZ - 1
    f32, bf16 = jnp.float32, jnp.bfloat16
    vmem = pl.BlockSpec(memory_space=pltpu.VMEM)
    hbm = pl.BlockSpec(memory_space=pl.ANY)
    dma = pltpu.SemaphoreType.DMA
    resp0, resp1, vgrad0, vgrad1, gath = pl.pallas_call(
        functools.partial(body, factor),
        out_shape=[jax.ShapeDtypeStruct(plane, f32)] * 4
        + [jax.ShapeDtypeStruct((2, GX * GY, PIECE, 128), bf16)],
        in_specs=[hbm, hbm, hbm],
        out_specs=[vmem] * 5,
        scratch_shapes=[
            pltpu.VMEM(flat, f32),
            pltpu.VMEM(flat, f32),
            pltpu.VMEM((27, C * C), f32),
            pltpu.VMEM((C * 32, 128), f32),
            pltpu.VMEM((TALL, 9 * C), bf16),
            pltpu.VMEM((TALL, 9 * C), bf16),
            pltpu.VMEM(grid, bf16),
            pltpu.VMEM(grid, bf16),
            pltpu.VMEM((NXL, NYL, TALL + 16, NZ), bf16),
            pltpu.VMEM((ROWS, 128), f32),
            pltpu.VMEM((GX, GY * PIECE, 128), bf16),
            pltpu.VMEM((GX, GY * PIECE, 128), bf16),
            pltpu.VMEM((peers, PIECE, 128), bf16),
            pltpu.VMEM((peers, PIECE, 128), bf16),
            pltpu.VMEM((PIECE, 128), f32),
            pltpu.VMEM((GZ, PIECE, 128), bf16),
            dma((3,)),
            dma((2, 10)),
            dma((2, 10)),
            dma((GX,)),
            dma((GX,)),
            dma((peers,)),
            dma((peers,)),
            dma((along,)),
            dma((along,)),
            dma((peers,)),
            dma((peers,)),
            dma((GX,)),
            dma((GX,)),
        ],
        compiler_params=pltpu.CompilerParams(
            collective_id=0, has_side_effects=True, vmem_limit_bytes=50 * 1024 * 1024
        ),
    )(volume.reshape(flat), upstream.reshape(flat), filters)
    finished = pl.pallas_call(
        finish,
        out_shape=[
            jax.ShapeDtypeStruct((C, NXL, NYL, NZ), f32),
            jax.ShapeDtypeStruct((C, NXL, NYL, NZ), f32),
            jax.ShapeDtypeStruct((27, C * C), f32),
            jax.ShapeDtypeStruct((1, C), f32),
        ],
        in_specs=[vmem] * 6,
        out_specs=[hbm, hbm, hbm, vmem],
        scratch_shapes=[
            pltpu.VMEM((C, NYL, NZ), f32),
            pltpu.VMEM((C, NYL, NZ), f32),
            pltpu.VMEM((C, NZ), f32),
            pltpu.VMEM((C * TAPS, 128), f32),
            pltpu.VMEM((27, C * C), f32),
            dma((7,)),
        ],
        compiler_params=pltpu.CompilerParams(vmem_limit_bytes=16 * 1024 * 1024),
    )(offsets.reshape(1, C), *(one.reshape(C, NYL, NZ) for one in (resp0, resp1, vgrad0, vgrad1)), gath.reshape(ROWS, 128))
    resp, vgrad, filter_grad, offset_grad = finished
    return (resp, vgrad, filter_grad, offset_grad.reshape(C))


def solution(mesh):
    placed = (P(None, "chan", "space", None), P(), P(), P(None, "chan", "space", None))
    return jax.shard_map(
        on_device,
        mesh=mesh,
        in_specs=placed,
        out_specs=(P(None, "chan", "space", None), P(None, "chan", "space", None), P(), P()),
        check_vma=False,
    )
```
